256 devices in a mesh: section: 8 (over z), expert: 16 (over y, x), dp: 2 (over core).
Axes of the slice: x: 4, y: 4, z: 8, core: 2. Of those that a mesh axis runs over, the one named last changes fastest.
Arguments:
- acts: bfloat16 [8, 3, 2048, 1024], P('section', None, ('expert', 'dp')), may hold values from -6 to 6
- out_grad: bfloat16 [3, 2048, 1024], P(None, ('expert', 'dp')), may hold values from -6 to 6
- ln_gain: float32 [8, 1024], P('section'), may hold values from 0.1 to 1.9
- router: bfloat16 [8, 1024, 16], P('section'), may hold values from -0.1875 to 0.1875
- w_in: bfloat16 [8, 16, 1024, 4096], P('section', 'expert', None, 'dp'), may hold values from -0.1875 to 0.1875
- w_out: bfloat16 [8, 16, 4096, 1024], P('section', 'expert', 'dp'), may hold values from -0.09375 to 0.09375
- expert_ids: int32 [8, 3, 2048, 2], P('section', None, ('expert', 'dp')), may hold values from 0 to 15, as said below
- slot_ids: int32 [8, 3, 2048, 2], P('section', None, ('expert', 'dp')), may hold values from 0 to 9, as said below
- capacity: int32 [8, 3, 16], P('section'), may hold values from 5 to 10
Outputs:
- in_grads: bfloat16 [8, 3, 2048, 1024], P('section', None, ('expert', 'dp'))
- gain_grad: float32 [8, 1024], P('section')
- router_grad: float32 [8, 1024, 16], P('section')
The draws below stay inside these ranges and needn't reach their ends.
Inputs may be any that keep to these rules, and one draw needn't show every extreme that they name: `expert_ids`: A token's two experts differ. `slot_ids`: within one block, micro-batch and aligned block of 64 tokens (the tokens of one device), the choices that name one expert hold the slots 0, 1, 2, ... without gaps, at most 10 of them; in every block and micro-batch one expert has 10 choices from every aligned block and capacity 10.
All inputs are finite; a program needn't handle non-finite values.
Results may differ from the reference program's by a relative error of at most 0.03.
Values may be sent and summed in bfloat16 or wider, within the bound.
A program may use at most 128 MiB of HBM per device.

```python
import math
import jax
import jax.numpy as jnp
from jax import lax

D = 1024
H = 4096
TOP = 2
MB = 3
TOK_DEV = 64
SECTIONS = 8
EXPERTS = 16
TOKENS = 2048
CAP = 10


def route_tables(key):
    base_key = jax.random.fold_in(key, 1001)
    key_full, key_cap, key_order, key_tok, key_limit = jax.random.split(base_key, 5)
    block_count = TOKENS // TOK_DEV
    columns = jnp.arange(EXPERTS, dtype=jnp.int32)
    full_expert = jax.random.randint(key_full, (SECTIONS, MB), 0, EXPERTS, dtype=jnp.int32)
    is_full = columns[None, None, None, :] == full_expert[:, :, None, None]
    lower_cap = CAP - CAP // 5
    load_caps = jax.random.randint(key_cap, (SECTIONS, MB, block_count, EXPERTS), lower_cap, CAP + 1, dtype=jnp.int32)
    load_caps = jnp.where(is_full, CAP, load_caps)
    order_score = jax.random.randint(key_order, (SECTIONS, MB, block_count, EXPERTS), 0, 1 << 20, dtype=jnp.int32) * EXPERTS + columns
    order_score = jnp.where(is_full, -1, order_score)
    expert_order = jnp.argsort(order_score, axis=-1, stable=True).astype(jnp.int32)
    ordered_caps = jnp.take_along_axis(load_caps, expert_order, axis=-1)
    load_ends = jnp.cumsum(ordered_caps, axis=-1)
    load_starts = load_ends - ordered_caps
    total_choices = TOP * TOK_DEV
    load_used = jnp.clip(total_choices - load_starts, 0, ordered_caps)
    used_ends = jnp.cumsum(load_used, axis=-1)
    used_starts = used_ends - load_used
    layout = jnp.arange(total_choices, dtype=jnp.int32)
    group_index = jnp.sum((used_ends[..., None, :] <= layout[:, None]).astype(jnp.int32), axis=-1)
    expert_at = jnp.take_along_axis(expert_order, group_index, axis=-1)
    slot_at = layout - jnp.take_along_axis(used_starts, group_index, axis=-1)
    token_score = jax.random.randint(key_tok, (SECTIONS, MB, block_count, TOK_DEV), 0, 1 << 20, dtype=jnp.int32) * TOK_DEV + jnp.arange(TOK_DEV, dtype=jnp.int32)
    token_perm = jnp.argsort(token_score, axis=-1, stable=True).astype(jnp.int32)
    token_place = jnp.argsort(token_perm, axis=-1, stable=True).astype(jnp.int32)
    layout_index = token_place[..., None] + jnp.arange(TOP, dtype=jnp.int32) * TOK_DEV
    layout_flat = layout_index.reshape(SECTIONS, MB, block_count, TOK_DEV * TOP)
    selected_expert_index = jnp.take_along_axis(expert_at, layout_flat, axis=-1).reshape(SECTIONS, MB, TOKENS, TOP)
    chosen_slots = jnp.take_along_axis(slot_at, layout_flat, axis=-1).reshape(SECTIONS, MB, TOKENS, TOP)
    limits = jax.random.randint(key_limit, (SECTIONS, MB, EXPERTS), CAP // 2, CAP + 1, dtype=jnp.int32)
    limits = jnp.where(columns[None, None, :] == full_expert[:, :, None], CAP, limits)
    return (selected_expert_index.astype(jnp.int32), chosen_slots.astype(jnp.int32), limits.astype(jnp.int32))


def draw_expert_ids(key, part):
    return route_tables(key)[0]


def draw_slot_ids(key, part):
    return route_tables(key)[1]


def draw_capacity(key, part):
    return route_tables(key)[2]


def steps_of(stream_key, extent, cuts, least, largest):
    def one(axis_at, blocks):
        heights = jax.random.uniform(jax.random.fold_in(jax.random.fold_in(stream_key, 6), axis_at), (blocks,), jnp.float32, least / len(cuts), largest / len(cuts))
        return jnp.repeat(jnp.exp(heights), extent[axis_at] // blocks).reshape((-1,) + (1,) * (len(extent) - axis_at - 1))

    level = one(*cuts[0])
    for cut in cuts[1:]:
        level = level * one(*cut)
    return level


def normal_values(own_key, dims, scale, most, cuts=(), held_as=jnp.bfloat16):
    drawn = scale * jax.random.normal(own_key, dims, jnp.float32)
    if cuts:
        drawn = drawn * steps_of(own_key, dims, cuts, -0.22, 0.18)
    return jnp.clip(drawn, -most, most).astype(held_as)


def setup_inputs(seed: int = 0) -> dict:
    key_list = jax.random.split(jax.random.key(seed), 10)
    return {
        "acts": normal_values(key_list[0], (SECTIONS, MB, TOKENS, D), 1.0, 6.0, ((0, 8), (2, 32))),
        "out_grad": normal_values(key_list[1], (MB, TOKENS, D), 1.0, 6.0, ((1, 32),)),
        "ln_gain": jnp.clip(1.0 + 0.18 * jax.random.normal(key_list[2], (SECTIONS, D), jnp.float32), 0.1, 1.9),
        "router": normal_values(key_list[3], (SECTIONS, D, EXPERTS), D ** -0.5, 0.1875, ((0, 8),)),
        "w_in": normal_values(key_list[4], (SECTIONS, EXPERTS, D, H), D ** -0.5, 0.1875, ((0, 8), (1, 16), (3, 2))),
        "w_out": normal_values(key_list[5], (SECTIONS, EXPERTS, H, D), H ** -0.5, 0.09375, ((0, 8), (1, 16), (2, 2))),
        "expert_ids": draw_expert_ids(jax.random.fold_in(key_list[9], 71), 0),
        "slot_ids": draw_slot_ids(jax.random.fold_in(key_list[9], 71), 0),
        "capacity": draw_capacity(jax.random.fold_in(key_list[9], 71), 0),
    }


GELU_C = math.sqrt(2.0 / math.pi)
PRECISE = lax.Precision.HIGHEST

def gelu_pair(hidden):
    inner_arg = GELU_C * (hidden + 0.044715 * hidden * hidden * hidden)
    tanh_val = jnp.tanh(inner_arg)
    active = 0.5 * hidden * (1.0 + tanh_val)
    gelu_slope = 0.5 * (1.0 + tanh_val) + 0.5 * hidden * (1.0 - tanh_val * tanh_val) * GELU_C * (1.0 + 3.0 * 0.044715 * hidden * hidden)
    return (active, gelu_slope)

def token_forward(inputs, norm_scale_weight, router_w):
    values = inputs.astype(jnp.float32)
    centred = values - lax.optimization_barrier(jnp.mean(values, axis=-1, keepdims=True))
    inverse_deviation = lax.rsqrt(lax.optimization_barrier(jnp.mean(centred * centred, axis=-1, keepdims=True)) + 1e-06)
    expert_unit_rows = centred * inverse_deviation
    normed = (expert_unit_rows * norm_scale_weight).astype(jnp.bfloat16)
    logits = jnp.dot(normed, router_w, preferred_element_type=jnp.float32)
    return (expert_unit_rows, inverse_deviation, normed, logits)

def gate_pair(chosen):
    first_gate = 1.0 / (1.0 + jnp.exp(chosen[:, 1] - chosen[:, 0]))
    return jnp.stack([first_gate, 1.0 - first_gate], axis=1)

def token_backward(grad_out, expert_unit_rows, inverse_deviation, normed, norm_scale_weight, router_w, gate_vals, pick_table, gate_dots, expert_part):
    gate_diff = gate_vals[:, 0] * gate_vals[:, 1] * (gate_dots[:, 0] - gate_dots[:, 1])
    dlogits = gate_diff[:, None] * (pick_table[:, 0, :] - pick_table[:, 1, :])
    norm_gradient = expert_part + jnp.dot(dlogits, router_w.astype(jnp.float32).T, precision=PRECISE)
    router_term = jnp.dot(normed.astype(jnp.float32).T, dlogits, precision=PRECISE)
    gain_term = lax.optimization_barrier(jnp.sum(norm_gradient * expert_unit_rows, axis=0))
    normalized_input_gradient = norm_gradient * norm_scale_weight
    input_gradient = inverse_deviation * (normalized_input_gradient - lax.optimization_barrier(jnp.mean(normalized_input_gradient, axis=-1, keepdims=True)) - expert_unit_rows * lax.optimization_barrier(jnp.mean(normalized_input_gradient * expert_unit_rows, axis=-1, keepdims=True)))
    in_grad = (grad_out.astype(jnp.float32) + input_gradient).astype(jnp.bfloat16)
    return (in_grad, gain_term, router_term)

def expert_backward(rows_u, rows_grad, first_proj, second_proj):
    hidden = jnp.dot(rows_u, first_proj, preferred_element_type=jnp.float32)
    active, gelu_slope = gelu_pair(hidden)
    back_grad = jnp.dot(rows_grad, second_proj.T, preferred_element_type=jnp.float32)
    gate_dot = lax.optimization_barrier(jnp.sum(active * back_grad, axis=-1)).astype(jnp.bfloat16)
    pre_grad = (back_grad * gelu_slope).astype(jnp.bfloat16)
    slot_grad = jnp.dot(pre_grad, first_proj.T, preferred_element_type=jnp.float32).astype(jnp.bfloat16)
    return (slot_grad, gate_dot)

def reference(acts, out_grad, ln_gain, router, w_in, w_out, expert_ids, slot_ids, capacity):
    block_count = TOKENS // TOK_DEV
    dump_row = block_count * EXPERTS * CAP
    block_of = jnp.arange(TOKENS, dtype=jnp.int32) // TOK_DEV
    columns = jnp.arange(EXPERTS, dtype=jnp.int32)
    grad_scale = 1.0 / math.sqrt(MB * TOKENS)
    incoming = [out_grad[micro_index] for micro_index in range(MB)]
    grads_all = [None] * SECTIONS
    gains_all = [None] * SECTIONS
    routers_all = [None] * SECTIONS
    for section_index in range(SECTIONS - 1, -1, -1):
        gain_sum = jnp.zeros((D,), jnp.float32)
        router_sum = jnp.zeros((D, EXPERTS), jnp.float32)
        outgoing = []
        for micro_index in range(MB):
            grad_out = incoming[micro_index]
            selected_expert_index = expert_ids[section_index, micro_index]
            chosen_slots = slot_ids[section_index, micro_index]
            expert_unit_rows, inverse_deviation, normed, logits = token_forward(acts[section_index, micro_index], ln_gain[section_index], router[section_index])
            gate_vals = gate_pair(jnp.take_along_axis(logits, selected_expert_index, axis=1))
            kept_mask = chosen_slots < capacity[section_index, micro_index][selected_expert_index]
            flat_index = jnp.where(kept_mask, (block_of[:, None] * EXPERTS + selected_expert_index) * CAP + chosen_slots, dump_row).astype(jnp.int32)
            flat_list = flat_index.reshape(-1)
            rows_u = jnp.zeros((dump_row + 1, D), jnp.bfloat16).at[flat_list].set(jnp.repeat(normed, TOP, axis=0))[:dump_row]
            rows_grad = jnp.zeros((dump_row + 1, D), jnp.bfloat16).at[flat_list].set(jnp.repeat(grad_out, TOP, axis=0))[:dump_row]
            rows_u = rows_u.reshape(block_count, EXPERTS, CAP, D).transpose(1, 0, 2, 3).reshape(EXPERTS, block_count * CAP, D)
            rows_grad = rows_grad.reshape(block_count, EXPERTS, CAP, D).transpose(1, 0, 2, 3).reshape(EXPERTS, block_count * CAP, D)
            slot_grad, gate_dot = lax.map(lambda packed: expert_backward(packed[0], packed[1], packed[2], packed[3]), (rows_u, rows_grad, w_in[section_index], w_out[section_index]))
            slot_grad = slot_grad.reshape(EXPERTS, block_count, CAP, D).transpose(1, 0, 2, 3).reshape(dump_row, D)
            gate_dot = gate_dot.reshape(EXPERTS, block_count, CAP).transpose(1, 0, 2).reshape(dump_row)
            slot_grad = jnp.concatenate([slot_grad, jnp.zeros((1, D), jnp.bfloat16)], axis=0)
            gate_dot = jnp.concatenate([gate_dot, jnp.zeros((1,), jnp.bfloat16)], axis=0)
            picked_rows = slot_grad[flat_index].astype(jnp.float32)
            expert_part = lax.optimization_barrier(jnp.sum(gate_vals[:, :, None] * picked_rows, axis=1))
            gate_dots = gate_dot[flat_index].astype(jnp.float32)
            pick_table = (selected_expert_index[:, :, None] == columns).astype(jnp.float32)
            in_grad, gain_term, router_term = token_backward(grad_out, expert_unit_rows, inverse_deviation, normed, ln_gain[section_index], router[section_index], gate_vals, pick_table, gate_dots, expert_part)
            outgoing.append(in_grad)
            gain_sum = gain_sum + gain_term
            router_sum = router_sum + router_term
        grads_all[section_index] = jnp.stack(outgoing)
        gains_all[section_index] = gain_sum * grad_scale
        routers_all[section_index] = router_sum * grad_scale
        incoming = outgoing
    return (jnp.stack(grads_all), jnp.stack(gains_all), jnp.stack(routers_all))
```

```python
import functools
import math

import jax
import jax.numpy as jnp
from jax import lax
from jax.experimental import pallas as pl
from jax.experimental.pallas import tpu as pltpu
from jax.sharding import PartitionSpec as P

GELU_C = math.sqrt(2.0 / math.pi)
MESH = pl.DeviceIdType.MESH
BF = jnp.bfloat16
F32 = jnp.float32
SIDE = 4
LANES = 128


def plane_offsets():
    offs = [(k // SIDE, k % SIDE) for k in range(1, SIDE * SIDE)]
    far = lambda o: min(o[0], SIDE - o[0]) + min(o[1], SIDE - o[1])
    return sorted(offs, key=lambda o: -far(o))


def dot(a, b, ca=1, cb=0):
    return lax.dot_general(a, b, (((ca,), (cb,)), ((), ())), preferred_element_type=F32)


def iota(shape, dim):
    return lax.broadcasted_iota(jnp.int32, shape, dim)


def stack_chunks(x):
    return jnp.concatenate([x[:, c : c + LANES] for c in range(0, x.shape[1], LANES)], axis=0)


def spread_chunks(x, rows):
    return jnp.concatenate([x[r : r + rows] for r in range(0, x.shape[0], rows)], axis=1)


def kernel(
    acts, out_grad, gain, router_t, ids, codes, w_in_own, w_out_own,
    o_grads, o_gain, o_router,
    w_in, w_out, w_out_t, slope, active, pre, rows,
    su, ru, sy, ry, sg, rg, sr, rr, rz, sz,
    unit_s, inv_s, normed_s, ydiff_s, extra_s, pdg_s,
    send_main, send_tail, mix_main, mix_tail, diff_main, diff_tail,
    router_pad, perm, perm_t, eye, router_acc, gain_acc,
    fin_s, fin_r, fin_x, fin_y, fin_t, fin_g,
    w_local, w_send, w_recv,
    u_send, u_recv, y_send, y_recv, g_send, g_recv, r_send, r_recv, z_send, z_recv,
    f_send, f_recv,
    *, scale,
):
    sec = lax.axis_index("section")
    exp = lax.axis_index("expert")
    core = lax.axis_index("dp")
    sections = lax.axis_size("section")
    last = sections - 1
    col = exp // SIDE
    row = lax.rem(exp, SIDE)
    peers = [
        lax.rem(col + dy, SIDE) * SIDE + lax.rem(row + dx, SIDE) for dy, dx in plane_offsets()
    ]
    experts = SIDE * SIDE
    micros = acts.shape[0]
    toks = acts.shape[1]
    width = acts.shape[2]
    half = w_in_own.shape[1]

    own_in = pltpu.make_async_copy(w_in_own, w_in.at[:, pl.ds(0, half)], w_local.at[0])
    own_out = pltpu.make_async_copy(w_out_own, w_out.at[pl.ds(0, half), :], w_local.at[1])
    own_in.start()
    own_out.start()

    barrier = pltpu.get_barrier_semaphore()
    for p in peers:
        pl.semaphore_signal(barrier, inc=1, device_id=(sec, p, core), device_id_type=MESH)
    pl.semaphore_signal(barrier, inc=1, device_id=(sec, exp, 1 - core), device_id_type=MESH)

    @pl.when(sec < last)
    def _():
        pl.semaphore_signal(barrier, inc=1, device_id=(sec + 1, exp, core), device_id_type=MESH)

    @pl.when(sec > 0)
    def _():
        pl.semaphore_wait(barrier, experts + 1)

    @pl.when(sec == 0)
    def _():
        pl.semaphore_wait(barrier, experts)

    part_in = pltpu.make_async_remote_copy(
        src_ref=w_in_own, dst_ref=w_in.at[:, pl.ds(half, half)],
        send_sem=w_send.at[0], recv_sem=w_recv.at[0],
        device_id=(sec, exp, 1 - core), device_id_type=MESH,
    )
    part_out = pltpu.make_async_remote_copy(
        src_ref=w_out_own, dst_ref=w_out.at[pl.ds(half, half), :],
        send_sem=w_send.at[1], recv_sem=w_recv.at[1],
        device_id=(sec, exp, 1 - core), device_id_type=MESH,
    )
    part_in.start()
    part_out.start()

    def scatter(src, dst, m, send_sem, recv_sem):
        for p in peers:
            pltpu.make_async_remote_copy(
                src_ref=src.at[m, p], dst_ref=dst.at[m, exp],
                send_sem=send_sem.at[m], recv_sem=recv_sem.at[m],
                device_id=(sec, p, core), device_id_type=MESH,
            ).start()
        dst[m, exp] = src[m, exp]

    def all_of(buf, m, sem):
        part = buf.at[m, pl.ds(0, experts - 1)]
        return pltpu.make_async_copy(part, part, sem.at[m])

    def pack(buf, m, main, tail):
        main = main.reshape(experts, 8, width)
        for q in range(4):
            lo = main[:, :, 256 * q : 256 * q + LANES]
            hi = main[:, :, 256 * q + LANES : 256 * q + 256]
            buf[m, :, 16 * q : 16 * q + 16, :] = jnp.concatenate([lo, hi], axis=1).astype(BF)
        buf[m, :, 64:80, :] = tail.reshape(experts, 16, LANES).astype(BF)

    def unpack_main(buf, m):
        parts = []
        for q in range(4):
            t = buf[m, :, 16 * q : 16 * q + 16, :].astype(F32)
            parts.append(t[:, :8, :].reshape(experts * 8, LANES))
            parts.append(t[:, 8:, :].reshape(experts * 8, LANES))
        return jnp.concatenate(parts, axis=1).astype(BF)

    def tail_of(buf, m):
        return buf[m, :, 64:80, :].reshape(experts * 16, LANES)

    def to_slots(x, m, buf):
        pack(buf, m, dot(send_main[m], x), dot(send_tail[m], stack_chunks(x)))

    def to_rows(buf, m):
        rows[0 : experts * 8, :] = unpack_main(buf, m)
        t = dot(perm[...], tail_of(buf, m))
        rows[experts * 8 : experts * 10, :] = spread_chunks(t, experts * 2).astype(BF)

    def from_rows(res, m, buf):
        tail = stack_chunks(res[experts * 8 : experts * 10].astype(BF))
        pack(buf, m, res[0 : experts * 8], dot(perm_t[...], tail))

    def combine(buf, m, main_table, tail_table):
        main = dot(main_table[m], unpack_main(buf, m))
        tail = dot(tail_table[m], tail_of(buf, m))
        return main + spread_chunks(tail, toks)

    q = iota((256, 256), 0)
    r = iota((256, 256), 1)
    picked = ((q & 31) >> 1) * 16 + (q & 1) * 8 + (q >> 5)
    perm[...] = (r == picked).astype(F32).astype(BF)
    picked_t = ((r & 31) >> 1) * 16 + (r & 1) * 8 + (r >> 5)
    perm_t[...] = (q == picked_t).astype(F32).astype(BF)
    eye[...] = (q == r).astype(F32).astype(BF)
    router_pad[...] = jnp.zeros_like(router_pad)
    router_pad[0:experts, :] = router_t[...]
    router_acc[...] = jnp.zeros_like(router_acc)
    gain_acc[...] = jnp.zeros_like(gain_acc)

    def tokens_forward(m):
        x = acts[m].astype(F32)
        centred = x - jnp.mean(x, axis=-1, keepdims=True)
        inv = lax.rsqrt(jnp.mean(centred * centred, axis=-1, keepdims=True) + 1e-06)
        unit = centred * inv
        normed = (unit * gain[...]).astype(BF)
        unit_s[m] = unit
        inv_s[m] = jnp.broadcast_to(inv, (toks, LANES))
        normed_s[m] = normed
        code1 = codes[m, 0:1, :]
        code2 = codes[m, 1:2, :]
        slot_r = iota((128, LANES), 0)
        slot_code = (slot_r >> 3) * 16 + (slot_r & 7)
        hit = ((slot_code == code1) | (slot_code == code2)).astype(F32)
        send_main[m] = hit[:, :toks].astype(BF)
        wide1 = jnp.concatenate([code1] * 4, axis=1)
        wide2 = jnp.concatenate([code2] * 4, axis=1)
        tail_r = iota((256, 512), 0)
        tail_code = (tail_r >> 4) * 16 + 8 + ((tail_r >> 3) & 1)
        same = (iota((256, 512), 1) >> 6) == (tail_r & 7)
        hit = (((tail_code == wide1) | (tail_code == wide2)) & same).astype(F32)
        send_tail[m] = hit.astype(BF)
        to_slots(normed, m, su)
        scatter(su, ru, m, u_send, u_recv)
        logits = dot(router_t[...], jnp.concatenate([normed, normed], axis=0), 1, 1)
        id1 = ids[m, 0:1, :]
        id2 = ids[m, 1:2, :]
        e_r = iota((experts, LANES), 0)
        chosen1 = jnp.sum(jnp.where(e_r == id1, logits, 0.0), axis=0, keepdims=True)
        chosen2 = jnp.sum(jnp.where(e_r == id2, logits, 0.0), axis=0, keepdims=True)
        gate1 = 1.0 / (1.0 + jnp.exp(chosen2 - chosen1))
        gate2 = 1.0 - gate1
        line = iota((8, LANES), 0)
        lines = jnp.where(line == 0, code1.astype(F32), 0.0)
        lines = jnp.where(line == 1, code2.astype(F32), lines)
        lines = jnp.where(line == 2, id1.astype(F32), lines)
        lines = jnp.where(line == 3, id2.astype(F32), lines)
        lines = jnp.where(line == 4, gate1, lines)
        lines = jnp.where(line == 5, gate2, lines)
        lines = jnp.concatenate([lines, jnp.zeros((LANES - 8, LANES), F32)], axis=0)
        turned = jnp.transpose(lines)[:toks]
        c1 = turned[:, 0:1].astype(jnp.int32)
        c2 = turned[:, 1:2].astype(jnp.int32)
        i1 = turned[:, 2:3].astype(jnp.int32)
        i2 = turned[:, 3:4].astype(jnp.int32)
        g1 = turned[:, 4:5]
        g2 = turned[:, 5:6]
        e_l = iota((toks, LANES), 1)
        pdg_s[m] = g1 * g2 * ((e_l == i1).astype(F32) - (e_l == i2).astype(F32))
        slot_code = (e_l >> 3) * 16 + (e_l & 7)
        hit1 = (slot_code == c1).astype(F32)
        hit2 = (slot_code == c2).astype(F32)
        mix_main[m] = (g1 * hit1 + g2 * hit2).astype(BF)
        diff_main[m] = (hit1 - hit2).astype(BF)
        lane = iota((toks, 256), 1)
        tail_code = (lane >> 4) * 16 + 8 + ((lane >> 3) & 1)
        hit1 = (tail_code == c1).astype(F32)
        hit2 = (tail_code == c2).astype(F32)
        mixed = g1 * hit1 + g2 * hit2
        differ = hit1 - hit2
        for c in range(8):
            here = (lane & 7) == c
            mix_tail[m, toks * c : toks * c + toks, :] = jnp.where(here, mixed, 0.0).astype(BF)
            diff_tail[m, toks * c : toks * c + toks, :] = jnp.where(here, differ, 0.0).astype(BF)

    def experts_forward(m):
        all_of(ru, m, u_recv).wait()
        to_rows(ru, m)

        @pl.loop(0, 4)
        def _(n):
            cols = pl.ds(pl.multiple_of(n * 1024, 1024), 1024)
            hidden = dot(rows[...], w_in[:, cols])
            square = hidden * hidden
            tanh = jnp.tanh(GELU_C * hidden * (1.0 + 0.044715 * square))
            rise = 0.5 * (1.0 + tanh)
            active[:, cols] = (hidden * rise).astype(BF)
            bend = 0.5 * hidden * (1.0 - tanh * tanh) * (GELU_C + (3.0 * 0.044715 * GELU_C) * square)
            slope[m, :, cols] = (rise + bend).astype(BF)

    def experts_value(m):
        from_rows(dot(active[...], w_out[...]), m, sy)
        scatter(sy, ry, m, y_send, y_recv)

    def tokens_value(m):
        all_of(ry, m, y_recv).wait()
        ydiff_s[m] = combine(ry, m, diff_main, diff_tail)

    def tokens_send(m):
        to_slots(rz[m], m, sg)
        scatter(sg, rg, m, g_send, g_recv)

    def tokens_gate(m):
        dots = jnp.sum(ydiff_s[m] * rz[m].astype(F32), axis=1, keepdims=True)
        dlogits = (dots * pdg_s[m]).astype(BF)
        extra_s[...] = dot(dlogits, router_pad[...])
        router_acc[...] += dot(dlogits, normed_s[m], 0, 0)[:experts]

    def experts_backward(m, turned):
        all_of(rg, m, g_recv).wait()
        to_rows(rg, m)
        if turned:
            back = dot(rows[...], w_out_t[...])
        else:
            back = dot(rows[...], w_out[...], 1, 1)
        pre[...] = (back * slope[m].astype(F32)).astype(BF)
        if turned:
            res = dot(pre[...], w_out[...])
        else:
            res = dot(pre[...], w_in[...], 1, 1)
        from_rows(res, m, sr)
        scatter(sr, rr, m, r_send, r_recv)

    def tokens_backward(m):
        all_of(rr, m, r_recv).wait()
        unit = unit_s[m]
        norm_grad = combine(rr, m, mix_main, mix_tail) + extra_s[...]
        xhat = norm_grad * gain[...]
        mean1 = jnp.mean(xhat, axis=-1, keepdims=True)
        mean2 = jnp.mean(xhat * unit, axis=-1, keepdims=True)
        step = inv_s[m][:, 0:1] * (xhat - mean1 - unit * mean2)
        in_grad = (rz[m].astype(F32) + step).astype(BF)
        sz[m] = in_grad

        @pl.when(sec > 0)
        def _():
            z_copy(m).start()

        o_grads[m] = in_grad
        terms = (norm_grad * unit).reshape(toks // 8, 8, width)
        gain_acc[...] += jnp.sum(terms, axis=0)

    def z_copy(m):
        return pltpu.make_async_remote_copy(
            src_ref=sz.at[m], dst_ref=rz.at[m],
            send_sem=z_send.at[m], recv_sem=z_recv.at[m],
            device_id=(jnp.maximum(sec - 1, 0), exp, core), device_id_type=MESH,
        )

    @pl.when(sec == last)
    def _():
        @pl.loop(0, micros)
        def _(m):
            rz[m] = out_grad[m]
            tokens_forward(m)
            tokens_send(m)

            @pl.when(m == 0)
            def _():
                own_in.wait()
                part_in.wait_recv()

            experts_forward(m)

            @pl.when(m == 0)
            def _():
                own_out.wait()
                part_out.wait_recv()

            experts_value(m)
            experts_backward(m, False)
            tokens_value(m)
            tokens_gate(m)
            tokens_backward(m)

    @pl.when(sec < last)
    def _():
        pl.loop(0, micros)(tokens_forward)
        own_in.wait()
        part_in.wait_recv()
        own_out.wait()
        part_out.wait_recv()

        @pl.loop(0, micros)
        def _(m):
            experts_forward(m)
            experts_value(m)

        @pl.loop(0, width // 256)
        def _(n):
            lines = pl.ds(pl.multiple_of(n * 256, 256), 256)
            w_out_t[lines, :] = dot(eye[...], w_out[:, lines], 1, 1).astype(BF)

        @pl.loop(0, 2 * half // 256)
        def _(n):
            lines = pl.ds(pl.multiple_of(n * 256, 256), 256)
            w_out[lines, :] = dot(eye[...], w_in[:, lines], 1, 1).astype(BF)

        pl.loop(0, micros)(tokens_value)

        @pl.loop(0, micros)
        def _(m):
            z_copy(m).wait_recv()
            tokens_send(m)
            tokens_gate(m)
            experts_backward(m, True)
            tokens_backward(m)

    for j in range(experts):
        lines = slice(8 * (j // 8), 8 * (j // 8) + 8)
        cols = slice(LANES * (j % 8), LANES * (j % 8) + LANES)
        fin_s[0, j, 0:8, :] = router_acc[lines, cols]
        fin_s[0, j, 8:16, :] = gain_acc[:, cols] if j < 8 else jnp.zeros((8, LANES), F32)
    for p in peers:
        pltpu.make_async_remote_copy(
            src_ref=fin_s.at[0, p], dst_ref=fin_r.at[0, exp],
            send_sem=f_send.at[0], recv_sem=f_recv.at[0],
            device_id=(sec, p, core), device_id_type=MESH,
        ).start()
    fin_r[0, exp] = fin_s[0, exp]
    all_of(fin_r, 0, f_recv).wait()
    fin_x[...] = jnp.sum(fin_r[0], axis=0)
    pair = pltpu.make_async_remote_copy(
        src_ref=fin_x, dst_ref=fin_y, send_sem=f_send.at[1], recv_sem=f_recv.at[1],
        device_id=(sec, exp, 1 - core), device_id_type=MESH,
    )
    pair.start()
    pair.wait()
    fin_t[...] = (fin_x[...] + fin_y[...]) * scale
    for p in peers:
        pltpu.make_async_remote_copy(
            src_ref=fin_t, dst_ref=fin_g.at[0, exp],
            send_sem=f_send.at[2], recv_sem=f_recv.at[2],
            device_id=(sec, p, core), device_id_type=MESH,
        ).start()
    fin_g[0, exp] = fin_t[...]
    got = fin_g.at[0, pl.ds(0, experts - 1)]
    pltpu.make_async_copy(got, got, f_recv.at[2]).wait()
    for j in range(experts):
        lines = slice(8 * (j // 8), 8 * (j // 8) + 8)
        cols = slice(LANES * (j % 8), LANES * (j % 8) + LANES)
        o_router[lines, cols] = fin_g[0, j, 0:8, :]
        if j < 8:
            o_gain[:, cols] = jnp.sum(fin_g[0, j, 8:16, :], axis=0, keepdims=True)

    @pl.loop(0, micros)
    def _(m):
        all_of(su, m, u_send).wait()
        all_of(sy, m, y_send).wait()
        all_of(sg, m, g_send).wait()
        all_of(sr, m, r_send).wait()

        @pl.when(sec > 0)
        def _():
            z_copy(m).wait_send()

    all_of(fin_s, 0, f_send).wait()
    pltpu.make_async_copy(got, got, f_send.at[2]).wait()
    part_in.wait_send()
    part_out.wait_send()


def per_device(acts, out_grad, ln_gain, router, w_in, w_out, expert_ids, slot_ids, capacity):
    _, micros, toks, width = acts.shape
    experts = router.shape[2]
    half = w_in.shape[3]
    cap_slots = 10
    slots = experts * cap_slots
    tokens_all = toks * lax.axis_size("expert") * lax.axis_size("dp")
    scale = 1.0 / math.sqrt(micros * tokens_all)
    ids = jnp.transpose(expert_ids[0], (0, 2, 1))
    places = jnp.transpose(slot_ids[0], (0, 2, 1))
    columns = jnp.arange(experts, dtype=jnp.int32)
    caps = jnp.sum(
        jnp.where(ids[..., None] == columns, capacity[0][:, None, None, :], 0), axis=-1
    )
    codes = jnp.where(places < caps, ids * 16 + places, -1)
    codes = jnp.concatenate([codes, codes], axis=2)
    ids = jnp.concatenate([ids, ids], axis=2)
    vmem = pl.BlockSpec(memory_space=pltpu.VMEM)
    hbm = pl.BlockSpec(memory_space=pl.ANY)
    dma = pltpu.SemaphoreType.DMA
    tiles = (micros, experts, 80, LANES)
    grads, gain_out, router_out = pl.pallas_call(
        functools.partial(kernel, scale=scale),
        out_shape=(
            jax.ShapeDtypeStruct((micros, toks, width), BF),
            jax.ShapeDtypeStruct((1, width), F32),
            jax.ShapeDtypeStruct((experts, width), F32),
        ),
        in_specs=[vmem] * 6 + [hbm] * 2,
        out_specs=(vmem, vmem, vmem),
        scratch_shapes=[
            pltpu.VMEM((width, 2 * half), BF),
            pltpu.VMEM((2 * half, width), BF),
            pltpu.VMEM((width, 2 * half), BF),
            pltpu.VMEM((micros, slots, 2 * half), BF),
            pltpu.VMEM((slots, 2 * half), BF),
            pltpu.VMEM((slots, 2 * half), BF),
            pltpu.VMEM((slots, width), BF),
        ]
        + [pltpu.VMEM(tiles, BF)] * 8
        + [pltpu.VMEM((micros, toks, width), BF)] * 2
        + [
            pltpu.VMEM((micros, toks, width), F32),
            pltpu.VMEM((micros, toks, LANES), F32),
            pltpu.VMEM((micros, toks, width), BF),
            pltpu.VMEM((micros, toks, width), F32),
            pltpu.VMEM((toks, width), F32),
            pltpu.VMEM((micros, toks, LANES), F32),
            pltpu.VMEM((micros, 128, toks), BF),
            pltpu.VMEM((micros, 256, 512), BF),
            pltpu.VMEM((micros, toks, 128), BF),
            pltpu.VMEM((micros, 512, 256), BF),
            pltpu.VMEM((micros, toks, 128), BF),
            pltpu.VMEM((micros, 512, 256), BF),
            pltpu.VMEM((LANES, width), BF),
            pltpu.VMEM((256, 256), BF),
            pltpu.VMEM((256, 256), BF),
            pltpu.VMEM((256, 256), BF),
            pltpu.VMEM((experts, width), F32),
            pltpu.VMEM((8, width), F32),
            pltpu.VMEM((1, experts, 16, LANES), F32),
            pltpu.VMEM((1, experts, 16, LANES), F32),
            pltpu.VMEM((16, LANES), F32),
            pltpu.VMEM((16, LANES), F32),
            pltpu.VMEM((16, LANES), F32),
            pltpu.VMEM((1, experts, 16, LANES), F32),
            dma((2,)),
            dma((2,)),
            dma((2,)),
        ]
        + [dma((micros,))] * 10
        + [dma((3,))] * 2,
        compiler_params=pltpu.CompilerParams(
            collective_id=0, has_side_effects=True, vmem_limit_bytes=60 * 2**20
        ),
    )(
        acts[0],
        out_grad,
        ln_gain,
        jnp.transpose(router[0]),
        ids,
        codes,
        w_in[0, 0],
        w_out[0, 0],
    )
    return (grads[None], gain_out, jnp.transpose(router_out)[None])


def solution(mesh):
    return jax.shard_map(
        per_device,
        mesh=mesh,
        in_specs=(
            P("section", None, ("expert", "dp"), None),
            P(None, ("expert", "dp"), None),
            P("section", None),
            P("section", None, None),
            P("section", "expert", None, "dp"),
            P("section", "expert", "dp", None),
            P("section", None, ("expert", "dp"), None),
            P("section", None, ("expert", "dp"), None),
            P("section", None, None),
        ),
        out_specs=(
            P("section", None, ("expert", "dp"), None),
            P("section", None),
            P("section", None, None),
        ),
        check_vma=False,
    )
```

```python
import functools
import math

import jax
import jax.numpy as jnp
from jax import lax
from jax.experimental import pallas as pl
from jax.experimental.pallas import tpu as pltpu
from jax.sharding import PartitionSpec as P

GELU_C = math.sqrt(2.0 / math.pi)
MESH = pl.DeviceIdType.MESH
BF = jnp.bfloat16
F32 = jnp.float32
SIDE = 4
LANES = 128


def plane_offsets():
    offs = [(k // SIDE, k % SIDE) for k in range(1, SIDE * SIDE)]
    far = lambda o: min(o[0], SIDE - o[0]) + min(o[1], SIDE - o[1])
    return sorted(offs, key=lambda o: -far(o))


def dot(a, b, ca=1, cb=0):
    return lax.dot_general(a, b, (((ca,), (cb,)), ((), ())), preferred_element_type=F32)


def iota(shape, dim):
    return lax.broadcasted_iota(jnp.int32, shape, dim)


def stack_chunks(x):
    return jnp.concatenate([x[:, c : c + LANES] for c in range(0, x.shape[1], LANES)], axis=0)


def spread_chunks(x, rows):
    return jnp.concatenate([x[r : r + rows] for r in range(0, x.shape[0], rows)], axis=1)


def kernel(
    acts, out_grad, gain, router_t, ids, places, caps, w_in_own, w_out_own,
    o_grads, o_gain, o_router,
    w_in, w_out, w_out_t, slope, active, pre, rows, back_s,
    su, ru, sg, rg, sy, ry, sr, rr, rz, sz,
    unit_s, inv_s, normed_s, ydiff_s, extra_s, pdg_s,
    send_main, send_tail, mix_main, mix_tail, diff_main, diff_tail,
    router_pad, perm, perm_t, eye, router_acc, gain_acc,
    fin_s, fin_r, fin_x, fin_y, fin_t, fin_g, gain_x, gain_y, gain_t, gain_g,
    w_local, w_send, w_recv,
    u_send, u_recv, g_send, g_recv, z_send, z_recv, y_send, y_recv, r_send, r_recv,
    f_send, f_recv,
    *, scale,
):
    sec = lax.axis_index("section")
    exp = lax.axis_index("expert")
    core = lax.axis_index("dp")
    sections = lax.axis_size("section")
    last = sections - 1
    col = exp // SIDE
    row = lax.rem(exp, SIDE)
    peers = [
        lax.rem(col + dy, SIDE) * SIDE + lax.rem(row + dx, SIDE) for dy, dx in plane_offsets()
    ]
    experts = SIDE * SIDE
    micros = acts.shape[0]
    toks = acts.shape[1]
    width = acts.shape[2]
    half = w_in_own.shape[1]

    own_in = pltpu.make_async_copy(w_in_own, w_in.at[:, pl.ds(0, half)], w_local.at[0])
    own_out = pltpu.make_async_copy(w_out_own, w_out.at[pl.ds(0, half), :], w_local.at[1])
    own_in.start()
    own_out.start()

    barrier = pltpu.get_barrier_semaphore()
    for p in peers:
        pl.semaphore_signal(barrier, inc=1, device_id=(sec, p, core), device_id_type=MESH)
    pl.semaphore_signal(barrier, inc=1, device_id=(sec, exp, 1 - core), device_id_type=MESH)

    @pl.when(sec < last)
    def _():
        pl.semaphore_signal(barrier, inc=1, device_id=(sec + 1, exp, core), device_id_type=MESH)

    part_in = pltpu.make_async_remote_copy(
        src_ref=w_in_own, dst_ref=w_in.at[:, pl.ds(half, half)],
        send_sem=w_send.at[0], recv_sem=w_recv.at[0],
        device_id=(sec, exp, 1 - core), device_id_type=MESH,
    )
    part_out = pltpu.make_async_remote_copy(
        src_ref=w_out_own, dst_ref=w_out.at[pl.ds(half, half), :],
        send_sem=w_send.at[1], recv_sem=w_recv.at[1],
        device_id=(sec, exp, 1 - core), device_id_type=MESH,
    )

    def scatter(src_of, dst_of, send_sem, recv_sem):
        for p in peers:
            pltpu.make_async_remote_copy(
                src_ref=src_of(p), dst_ref=dst_of(exp), send_sem=send_sem, recv_sem=recv_sem,
                device_id=(sec, p, core), device_id_type=MESH,
            ).start()

    def others(part, sem):
        return pltpu.make_async_copy(part, part, sem)

    def all_parts(buf, m, h, sem):
        return others(buf.at[m, h, pl.ds(0, experts - 1)], sem.at[m, h])

    def all_rows(buf, m, sem):
        return others(buf.at[m, pl.ds(0, experts - 1)], sem.at[m])

    def send_part(src, dst, m, h, send_sem, recv_sem):
        scatter(
            lambda p: src.at[m, h, p], lambda p: dst.at[m, h, p],
            send_sem.at[m, h], recv_sem.at[m, h],
        )
        dst[m, h, exp] = src[m, h, exp]

    def send_rows(src, dst, m, lines, send_sem, recv_sem):
        scatter(
            lambda p: src.at[m, p, lines], lambda p: dst.at[m, p, lines],
            send_sem.at[m], recv_sem.at[m],
        )
        dst[m, exp, lines] = src[m, exp, lines]

    def two_tiles(main):
        main = main.reshape(experts, 8, 4 * LANES)
        return [
            jnp.concatenate([main[:, :, c : c + LANES], main[:, :, c + LANES : c + 2 * LANES]], axis=1).astype(BF)
            for c in (0, 2 * LANES)
        ]

    def from_tiles(tiles):
        parts = []
        for t in tiles:
            t = t.astype(F32)
            parts.append(t[:, :8, :].reshape(experts * 8, LANES))
            parts.append(t[:, 8:, :].reshape(experts * 8, LANES))
        return jnp.concatenate(parts, axis=1).astype(BF)

    def to_slots(x, m, h, buf):
        tiles = two_tiles(dot(send_main[m], x))
        buf[m, h, :, 0:16, :] = tiles[0]
        buf[m, h, :, 16:32, :] = tiles[1]
        tail = dot(send_tail[m], stack_chunks(x))
        buf[m, h, :, 32:48, :] = tail.reshape(experts, 16, LANES).astype(BF)

    def to_rows(buf, m, h):
        cols = slice(512 * h, 512 * h + 512)
        rows[0 : experts * 8, cols] = from_tiles([buf[m, h, :, 0:16, :], buf[m, h, :, 16:32, :]])
        t = dot(perm[...], buf[m, h, :, 32:48, :].reshape(experts * 16, LANES))
        rows[experts * 8 : experts * 10, cols] = spread_chunks(t, experts * 2).astype(BF)

    def from_rows(product, m, buf, dst, send_sem, recv_sem):
        tails = []
        for h in range(2):
            res = product(slice(512 * h, 512 * h + 512))
            tiles = two_tiles(res[0 : experts * 8])
            buf[m, :, 32 * h : 32 * h + 16, :] = tiles[0]
            buf[m, :, 32 * h + 16 : 32 * h + 32, :] = tiles[1]
            tails.append(stack_chunks(res[experts * 8 : experts * 10].astype(BF)))
            if h == 0:
                send_rows(buf, dst, m, pl.ds(0, 32), send_sem, recv_sem)
        tail = dot(perm_t[...], jnp.concatenate(tails, axis=0))
        buf[m, :, 64:80, :] = tail.reshape(experts, 16, LANES).astype(BF)
        send_rows(buf, dst, m, pl.ds(32, 48), send_sem, recv_sem)

    def combine(buf, m, main_table, tail_table):
        tiles = [buf[m, :, 16 * q : 16 * q + 16, :] for q in range(4)]
        main = dot(main_table[m], from_tiles(tiles))
        tail = dot(tail_table[m], buf[m, :, 64:80, :].reshape(experts * 16, LANES))
        return main + spread_chunks(tail, toks)

    def grad_of(m):
        return jnp.concatenate([rz[m, 0], rz[m, 1]], axis=1)

    q = iota((256, 256), 0)
    r = iota((256, 256), 1)
    q_half = iota((128, 256), 0)
    picked = ((q_half & 31) >> 1) * 16 + (q_half & 1) * 4 + (q_half >> 5)
    perm[...] = (iota((128, 256), 1) == picked).astype(F32).astype(BF)
    picked_t = ((r & 31) >> 1) * 16 + (r & 1) * 8 + (r >> 5)
    perm_t[...] = (q == picked_t).astype(F32).astype(BF)
    eye[...] = (q == r).astype(F32).astype(BF)
    router_pad[...] = jnp.zeros_like(router_pad)
    router_pad[0:experts, :] = router_t[...]
    router_acc[...] = jnp.zeros_like(router_acc)
    gain_acc[...] = jnp.zeros_like(gain_acc)

    e_r = iota((experts, LANES), 0)

    def twice(line):
        return jnp.concatenate([line, line], axis=1)

    def code_lines(m):
        square = iota((experts, experts), 0) == iota((experts, experts), 1)
        limit = jnp.sum(jnp.where(square, caps[m].astype(F32), 0.0), axis=1, keepdims=True)
        found = []
        for k in range(2):
            chosen = twice(ids[m, k : k + 1, :])
            place = twice(places[m, k : k + 1, :])
            most = jnp.sum(jnp.where(e_r == chosen, limit, 0.0), axis=0, keepdims=True)
            found += [chosen, jnp.where(place.astype(F32) < most, chosen * 16 + place, -1)]
        return found

    def tokens_forward(m):
        x = acts[m].astype(F32)
        centred = x - jnp.mean(x, axis=-1, keepdims=True)
        inv = lax.rsqrt(jnp.mean(centred * centred, axis=-1, keepdims=True) + 1e-06)
        unit = centred * inv
        normed = (unit * gain[...]).astype(BF)
        unit_s[m] = unit
        inv_s[m] = jnp.broadcast_to(inv, (toks, LANES))
        normed_s[m] = normed
        _, code1, _, code2 = code_lines(m)
        slot_r = iota((128, LANES), 0)
        slot_code = (slot_r >> 3) * 16 + (slot_r & 7)
        hit = ((slot_code == code1) | (slot_code == code2)).astype(F32)
        send_main[m] = hit[:, :toks].astype(BF)
        wide1 = jnp.concatenate([code1] * 2, axis=1)
        wide2 = jnp.concatenate([code2] * 2, axis=1)
        tail_r = iota((256, 256), 0)
        tail_code = (tail_r >> 4) * 16 + 8 + ((tail_r >> 2) & 1)
        same = ((iota((256, 256), 1) >> 6) == (tail_r & 3)) & ((tail_r & 8) == 0)
        hit = (((tail_code == wide1) | (tail_code == wide2)) & same).astype(F32)
        send_tail[m] = hit.astype(BF)
        for h in range(2):
            to_slots(normed[:, 512 * h : 512 * h + 512], m, h, su)

    def tokens_tables(m):
        id1, code1, id2, code2 = code_lines(m)
        normed = normed_s[m]
        logits = dot(router_t[...], jnp.concatenate([normed, normed], axis=0), 1, 1)
        chosen1 = jnp.sum(jnp.where(e_r == id1, logits, 0.0), axis=0, keepdims=True)
        chosen2 = jnp.sum(jnp.where(e_r == id2, logits, 0.0), axis=0, keepdims=True)
        gate1 = 1.0 / (1.0 + jnp.exp(chosen2 - chosen1))
        gate2 = 1.0 - gate1
        line = iota((8, LANES), 0)
        lines = jnp.where(line == 0, code1.astype(F32), 0.0)
        lines = jnp.where(line == 1, code2.astype(F32), lines)
        lines = jnp.where(line == 2, id1.astype(F32), lines)
        lines = jnp.where(line == 3, id2.astype(F32), lines)
        lines = jnp.where(line == 4, gate1, lines)
        lines = jnp.where(line == 5, gate2, lines)
        lines = jnp.concatenate([lines, jnp.zeros((LANES - 8, LANES), F32)], axis=0)
        turned = jnp.transpose(lines)[:toks]
        c1 = turned[:, 0:1].astype(jnp.int32)
        c2 = turned[:, 1:2].astype(jnp.int32)
        i1 = turned[:, 2:3].astype(jnp.int32)
        i2 = turned[:, 3:4].astype(jnp.int32)
        g1 = turned[:, 4:5]
        g2 = turned[:, 5:6]
        e_l = iota((toks, LANES), 1)
        pdg_s[m] = g1 * g2 * ((e_l == i1).astype(F32) - (e_l == i2).astype(F32))
        slot_code = (e_l >> 3) * 16 + (e_l & 7)
        hit1 = (slot_code == c1).astype(F32)
        hit2 = (slot_code == c2).astype(F32)
        mix_main[m] = (g1 * hit1 + g2 * hit2).astype(BF)
        diff_main[m] = (hit1 - hit2).astype(BF)
        lane = iota((toks, 256), 1)
        tail_code = (lane >> 4) * 16 + 8 + ((lane >> 3) & 1)
        hit1 = (tail_code == c1).astype(F32)
        hit2 = (tail_code == c2).astype(F32)
        mixed = g1 * hit1 + g2 * hit2
        differ = hit1 - hit2
        for c in range(8):
            here = (lane & 7) == c
            mix_tail[m, toks * c : toks * c + toks, :] = jnp.where(here, mixed, 0.0).astype(BF)
            diff_tail[m, toks * c : toks * c + toks, :] = jnp.where(here, differ, 0.0).astype(BF)

    def experts_forward(m):
        for h in range(2):
            all_parts(ru, m, h, u_recv).wait()
            to_rows(ru, m, h)
        for n in range(4):
            cols = slice(1024 * n, 1024 * n + 1024)
            hidden = dot(rows[...], w_in[:, cols])
            square = hidden * hidden
            tanh = jnp.tanh(GELU_C * hidden * (1.0 + 0.044715 * square))
            rise = 0.5 * (1.0 + tanh)
            active[m, :, cols] = (hidden * rise).astype(BF)
            bend = 0.5 * hidden * (1.0 - tanh * tanh) * (GELU_C + (3.0 * 0.044715 * GELU_C) * square)
            slope[m, :, cols] = (rise + bend).astype(BF)

    def experts_value(m):
        from_rows(lambda cols: dot(active[m], w_out[:, cols]), m, sy, ry, y_send, y_recv)

    def tokens_value(m):
        all_rows(ry, m, y_recv).wait()
        ydiff_s[m] = combine(ry, m, diff_main, diff_tail)

    def tokens_send(m, h):
        to_slots(rz[m, h], m, h, sg)
        send_part(sg, rg, m, h, g_send, g_recv)

    def tokens_gate(m):
        dots = jnp.sum(ydiff_s[m] * grad_of(m).astype(F32), axis=1, keepdims=True)
        dlogits = (dots * pdg_s[m]).astype(BF)
        extra_s[m] = dot(dlogits, router_pad[...])
        router_acc[...] += dot(dlogits, normed_s[m], 0, 0)[:experts]

    def experts_backward(m, turned):
        def product(h):
            cols = slice(512 * h, 512 * h + 512)
            if turned:
                return dot(rows[:, cols], w_out_t[cols, :])
            return dot(rows[:, cols], w_out[:, cols], 1, 1)

        all_parts(rg, m, 0, g_recv).wait()
        to_rows(rg, m, 0)
        back_s[...] = product(0)
        all_parts(rg, m, 1, g_recv).wait()
        to_rows(rg, m, 1)
        pre[...] = ((back_s[...] + product(1)) * slope[m].astype(F32)).astype(BF)

    def experts_return(m, turned):
        def product(cols):
            if turned:
                return dot(pre[...], w_out[:, cols])
            return dot(pre[...], w_in[cols, :], 1, 1)

        from_rows(product, m, sr, rr, r_send, r_recv)

    def tokens_backward(m):
        all_rows(rr, m, r_recv).wait()
        unit = unit_s[m]
        norm_grad = combine(rr, m, mix_main, mix_tail) + extra_s[m]
        xhat = norm_grad * gain[...]
        mean1 = jnp.mean(xhat, axis=-1, keepdims=True)
        mean2 = jnp.mean(xhat * unit, axis=-1, keepdims=True)
        step = inv_s[m][:, 0:1] * (xhat - mean1 - unit * mean2)
        in_grad = (grad_of(m).astype(F32) + step).astype(BF)
        for h in range(2):
            sz[m, h] = in_grad[:, 512 * h : 512 * h + 512]

            @pl.when(sec > 0)
            def _():
                z_copy(m, h).start()

        o_grads[m] = in_grad
        terms = (norm_grad * unit).reshape(toks // 8, 8, width)
        gain_acc[...] += jnp.sum(terms, axis=0)

    def z_copy(m, h):
        return pltpu.make_async_remote_copy(
            src_ref=sz.at[m, h], dst_ref=rz.at[m, h],
            send_sem=z_send.at[m, h], recv_sem=z_recv.at[m, h],
            device_id=(jnp.maximum(sec - 1, 0), exp, core), device_id_type=MESH,
        )

    def tile(j):
        lines = slice(8 * (j // 8), 8 * (j // 8) + 8)
        return lines, slice(LANES * (j % 8), LANES * (j % 8) + LANES)

    def to_peers(src_of, dst, k):
        scatter(src_of, lambda p: dst.at[p], f_send.at[k], f_recv.at[k])

    def to_pair(src, dst, k):
        return pltpu.make_async_remote_copy(
            src_ref=src, dst_ref=dst, send_sem=f_send.at[k], recv_sem=f_recv.at[k],
            device_id=(sec, exp, 1 - core), device_id_type=MESH,
        )

    def all_but_one(buf, sem, k):
        return others(buf.at[pl.ds(0, experts - 1)], sem.at[k])

    def router_parts():
        for j in range(experts):
            lines, cols = tile(j)
            fin_s[j] = router_acc[lines, cols]
        to_peers(lambda p: fin_s.at[p], fin_r, 0)
        fin_r[exp] = fin_s[exp]

    def router_sums():
        all_but_one(fin_r, f_recv, 0).wait()
        fin_x[...] = jnp.sum(fin_r[...], axis=0)
        pair = to_pair(fin_x, fin_y, 1)
        pair.start()
        pair.wait()
        fin_t[...] = (fin_x[...] + fin_y[...]) * scale
        to_peers(lambda p: fin_t, fin_g, 2)
        fin_g[exp] = fin_t[...]

    def gain_sums():
        gain_x[...] = jnp.sum(gain_acc[...], axis=0, keepdims=True)
        pair = to_pair(gain_x, gain_y, 3)
        pair.start()
        pair.wait()
        gain_t[...] = (gain_x[...] + gain_y[...]) * scale
        to_peers(lambda p: gain_t, gain_g, 4)
        gain_g[exp] = gain_t[...]

    tokens_forward(0)

    @pl.when(sec == last)
    def _():
        for m in range(micros):
            for h in range(2):
                rz[m, h] = out_grad[m, :, 512 * h : 512 * h + 512]
        for h in range(2):
            to_slots(rz[0, h], 0, h, sg)

    @pl.when(sec > 0)
    def _():
        pl.semaphore_wait(barrier, experts + 1)

    @pl.when(sec == 0)
    def _():
        pl.semaphore_wait(barrier, experts)

    part_in.start()
    for h in range(2):
        send_part(su, ru, 0, h, u_send, u_recv)

    @pl.when(sec == last)
    def _():
        for h in range(2):
            send_part(sg, rg, 0, h, g_send, g_recv)

    tokens_tables(0)

    @pl.loop(1, micros)
    def _(m):
        tokens_forward(m)
        for h in range(2):
            send_part(su, ru, m, h, u_send, u_recv)

        @pl.when(sec == last)
        def _():
            for h in range(2):
                tokens_send(m, h)

        tokens_tables(m)

    part_out.start()
    own_in.wait()
    part_in.wait_recv()
    pl.loop(0, micros)(experts_forward)
    own_out.wait()
    part_out.wait_recv()
    experts_value(0)

    @pl.when(sec == last)
    def _():
        experts_backward(0, False)
        experts_return(0, False)
        experts_value(1)
        tokens_value(0)
        tokens_gate(0)
        experts_backward(1, False)
        tokens_backward(0)
        experts_return(1, False)
        experts_value(2)
        tokens_value(1)
        tokens_gate(1)
        experts_backward(2, False)
        tokens_backward(1)
        experts_return(2, False)
        tokens_value(2)
        tokens_gate(2)
        router_parts()

    @pl.when(sec < last)
    def _():
        pl.loop(1, micros)(experts_value)

        @pl.loop(0, width // 256)
        def _(n):
            lines = pl.ds(pl.multiple_of(n * 256, 256), 256)
            w_out_t[lines, :] = dot(eye[...], w_out[:, lines], 1, 1).astype(BF)

        @pl.loop(0, 2 * half // 256)
        def _(n):
            lines = pl.ds(pl.multiple_of(n * 256, 256), 256)
            w_out[lines, :] = dot(eye[...], w_in[:, lines], 1, 1).astype(BF)

        pl.loop(0, micros)(tokens_value)

        @pl.loop(0, micros)
        def _(m):
            for h in range(2):
                z_copy(m, h).wait_recv()
                tokens_send(m, h)
            tokens_gate(m)

            @pl.when(m > 0)
            def _():
                tokens_backward(m - 1)

            @pl.when(m == micros - 1)
            def _():
                router_parts()

            experts_backward(m, True)
            experts_return(m, True)

    router_sums()
    tokens_backward(micros - 1)
    gain_sums()
    all_but_one(fin_g, f_recv, 2).wait()
    for j in range(experts):
        lines, cols = tile(j)
        o_router[lines, cols] = fin_g[j]
    all_but_one(gain_g, f_recv, 4).wait()
    o_gain[...] = jnp.sum(gain_g[...], axis=0)

    @pl.loop(0, micros)
    def _(m):
        all_rows(sy, m, y_send).wait()
        all_rows(sr, m, r_send).wait()
        for h in range(2):
            all_parts(su, m, h, u_send).wait()
            all_parts(sg, m, h, g_send).wait()

            @pl.when(sec > 0)
            def _():
                z_copy(m, h).wait_send()

    all_but_one(fin_r, f_send, 0).wait()
    all_but_one(fin_g, f_send, 2).wait()
    all_but_one(gain_g, f_send, 4).wait()
    part_in.wait_send()
    part_out.wait_send()


def copy_out(a, b, c, to_a, to_b, to_c):
    to_a[...] = a[...]
    to_b[...] = b[...]
    to_c[...] = c[...]


def per_device(acts, out_grad, ln_gain, router, w_in, w_out, expert_ids, slot_ids, capacity):
    _, micros, toks, width = acts.shape
    experts = router.shape[2]
    half = w_in.shape[3]
    cap_slots = 10
    slots = experts * cap_slots
    tokens_all = toks * lax.axis_size("expert") * lax.axis_size("dp")
    scale = 1.0 / math.sqrt(micros * tokens_all)
    ids = jnp.transpose(expert_ids[0], (0, 2, 1))
    places = jnp.transpose(slot_ids[0], (0, 2, 1))
    caps = jnp.transpose(capacity, (1, 0, 2))
    vmem = pl.BlockSpec(memory_space=pltpu.VMEM)
    hbm = pl.BlockSpec(memory_space=pl.ANY)
    dma = pltpu.SemaphoreType.DMA
    grads, gain_out, router_out = pl.pallas_call(
        functools.partial(kernel, scale=scale),
        out_shape=(
            jax.ShapeDtypeStruct((micros, toks, width), BF),
            jax.ShapeDtypeStruct((1, width), F32),
            jax.ShapeDtypeStruct((experts, width), F32),
        ),
        in_specs=[vmem] * 7 + [hbm] * 2,
        out_specs=(vmem, vmem, vmem),
        scratch_shapes=[
            pltpu.VMEM((width, 2 * half), BF),
            pltpu.VMEM((2 * half, width), BF),
            pltpu.VMEM((width, 2 * half), BF),
            pltpu.VMEM((micros, slots, 2 * half), BF),
            pltpu.VMEM((micros, slots, 2 * half), BF),
            pltpu.VMEM((slots, 2 * half), BF),
            pltpu.VMEM((slots, width), BF),
            pltpu.VMEM((slots, 2 * half), F32),
        ]
        + [pltpu.VMEM((micros, 2, experts, 48, LANES), BF)] * 4
        + [pltpu.VMEM((micros, experts, 80, LANES), BF)] * 4
        + [pltpu.VMEM((micros, 2, toks, width // 2), BF)] * 2
        + [
            pltpu.VMEM((micros, toks, width), F32),
            pltpu.VMEM((micros, toks, LANES), F32),
            pltpu.VMEM((micros, toks, width), BF),
            pltpu.VMEM((micros, toks, width), F32),
            pltpu.VMEM((micros, toks, width), F32),
            pltpu.VMEM((micros, toks, LANES), F32),
            pltpu.VMEM((micros, 128, toks), BF),
            pltpu.VMEM((micros, 256, 256), BF),
            pltpu.VMEM((micros, toks, 128), BF),
            pltpu.VMEM((micros, 512, 256), BF),
            pltpu.VMEM((micros, toks, 128), BF),
            pltpu.VMEM((micros, 512, 256), BF),
            pltpu.VMEM((LANES, width), BF),
            pltpu.VMEM((128, 256), BF),
            pltpu.VMEM((256, 256), BF),
            pltpu.VMEM((256, 256), BF),
            pltpu.VMEM((experts, width), F32),
            pltpu.VMEM((8, width), F32),
            pltpu.VMEM((experts, 8, LANES), F32),
            pltpu.VMEM((experts, 8, LANES), F32),
            pltpu.VMEM((8, LANES), F32),
            pltpu.VMEM((8, LANES), F32),
            pltpu.VMEM((8, LANES), F32),
            pltpu.VMEM((experts, 8, LANES), F32),
            pltpu.VMEM((1, width), F32),
            pltpu.VMEM((1, width), F32),
            pltpu.VMEM((1, width), F32),
            pltpu.VMEM((experts, 1, width), F32),
            dma((2,)),
            dma((2,)),
            dma((2,)),
        ]
        + [dma((micros, 2))] * 6
        + [dma((micros,))] * 4
        + [dma((5,))] * 2,
        compiler_params=pltpu.CompilerParams(
            collective_id=0, has_side_effects=True, vmem_limit_bytes=60 * 2**20
        ),
    )(
        acts[0],
        out_grad,
        ln_gain,
        jnp.transpose(router[0]),
        ids,
        places,
        caps,
        w_in[0, 0],
        w_out[0, 0],
    )
    grads, gain_out, router_out = pl.pallas_call(
        copy_out,
        out_shape=(
            jax.ShapeDtypeStruct((micros, toks, width), BF),
            jax.ShapeDtypeStruct((1, width), F32),
            jax.ShapeDtypeStruct((experts, width), F32),
        ),
        in_specs=[vmem] * 3,
        out_specs=(vmem, vmem, vmem),
    )(grads, gain_out, router_out)
    return (grads[None], gain_out, jnp.transpose(router_out)[None])


def solution(mesh):
    return jax.shard_map(
        per_device,
        mesh=mesh,
        in_specs=(
            P("section", None, ("expert", "dp"), None),
            P(None, ("expert", "dp"), None),
            P("section", None),
            P("section", None, None),
            P("section", "expert", None, "dp"),
            P("section", "expert", "dp", None),
            P("section", None, ("expert", "dp"), None),
            P("section", None, ("expert", "dp"), None),
            P("section", None, None),
        ),
        out_specs=(
            P("section", None, ("expert", "dp"), None),
            P("section", None),
            P("section", None, None),
        ),
        check_vma=False,
    )
```

```python
import functools
import math

import jax
import jax.numpy as jnp
from jax import lax
from jax.experimental import pallas as pl
from jax.experimental.pallas import tpu as pltpu
from jax.sharding import PartitionSpec as P

GELU_C = math.sqrt(2.0 / math.pi)
MESH = pl.DeviceIdType.MESH
BF = jnp.bfloat16
F32 = jnp.float32
SIDE = 4
LANES = 128


def plane_offsets():
    offs = [(k // SIDE, k % SIDE) for k in range(1, SIDE * SIDE)]
    far = lambda o: min(o[0], SIDE - o[0]) + min(o[1], SIDE - o[1])
    return sorted(offs, key=lambda o: -far(o))


def dot(a, b, ca=1, cb=0):
    return lax.dot_general(a, b, (((ca,), (cb,)), ((), ())), preferred_element_type=F32)


def iota(shape, dim):
    return lax.broadcasted_iota(jnp.int32, shape, dim)


def stack_chunks(x):
    return jnp.concatenate([x[:, c : c + LANES] for c in range(0, x.shape[1], LANES)], axis=0)


def spread_chunks(x, rows):
    return jnp.concatenate([x[r : r + rows] for r in range(0, x.shape[0], rows)], axis=1)


def kernel(
    acts, out_grad, gain, router_t, ids, places, caps, w_in_own, w_out_own,
    o_grads, o_gain, o_router,
    w_in, w_out, w_out_t, slope, active, pre, rows, back_s,
    su, ru, sg, rg, sy, ry, sr, rr, rz, sz,
    unit_s, inv_s, normed_s, ydiff_s, extra_s, pdg_s,
    send_main, send_tail, mix_main, mix_tail, diff_main, diff_tail,
    router_pad, perm, perm_t, eye, router_acc, gain_acc,
    fin_s, fin_r, fin_x, fin_y, fin_t, fin_g, gain_x, gain_y, gain_t, gain_g,
    w_local, w_send, w_recv,
    u_send, u_recv, g_send, g_recv, z_send, z_recv, y_send, y_recv, r_send, r_recv,
    f_send, f_recv,
    *, scale,
):
    sec = lax.axis_index("section")
    exp = lax.axis_index("expert")
    core = lax.axis_index("dp")
    sections = lax.axis_size("section")
    last = sections - 1
    col = exp // SIDE
    row = lax.rem(exp, SIDE)
    peers = [
        lax.rem(col + dy, SIDE) * SIDE + lax.rem(row + dx, SIDE) for dy, dx in plane_offsets()
    ]
    experts = SIDE * SIDE
    micros = acts.shape[0]
    toks = acts.shape[1]
    width = acts.shape[2]
    half = w_in_own.shape[1]

    own_in = pltpu.make_async_copy(w_in_own, w_in.at[:, pl.ds(0, half)], w_local.at[0])
    own_out = pltpu.make_async_copy(w_out_own, w_out.at[pl.ds(0, half), :], w_local.at[1])
    own_in.start()
    own_out.start()

    barrier = pltpu.get_barrier_semaphore()
    for p in peers:
        pl.semaphore_signal(barrier, inc=1, device_id=(sec, p, core), device_id_type=MESH)
    pl.semaphore_signal(barrier, inc=1, device_id=(sec, exp, 1 - core), device_id_type=MESH)

    @pl.when(sec < last)
    def _():
        pl.semaphore_signal(barrier, inc=1, device_id=(sec + 1, exp, core), device_id_type=MESH)

    part_in = pltpu.make_async_remote_copy(
        src_ref=w_in_own, dst_ref=w_in.at[:, pl.ds(half, half)],
        send_sem=w_send.at[0], recv_sem=w_recv.at[0],
        device_id=(sec, exp, 1 - core), device_id_type=MESH,
    )
    part_out = pltpu.make_async_remote_copy(
        src_ref=w_out_own, dst_ref=w_out.at[pl.ds(half, half), :],
        send_sem=w_send.at[1], recv_sem=w_recv.at[1],
        device_id=(sec, exp, 1 - core), device_id_type=MESH,
    )

    def scatter(src_of, dst_of, send_sem, recv_sem):
        for p in peers:
            pltpu.make_async_remote_copy(
                src_ref=src_of(p), dst_ref=dst_of(exp), send_sem=send_sem, recv_sem=recv_sem,
                device_id=(sec, p, core), device_id_type=MESH,
            ).start()

    def others(part, sem):
        return pltpu.make_async_copy(part, part, sem)

    def all_parts(buf, m, h, sem):
        return others(buf.at[m, h, pl.ds(0, experts - 1)], sem.at[m, h])

    def all_rows(buf, m, sem):
        return others(buf.at[m, pl.ds(0, experts - 1)], sem.at[m])

    def send_part(src, dst, m, h, send_sem, recv_sem):
        scatter(
            lambda p: src.at[m, h, p], lambda p: dst.at[m, h, p],
            send_sem.at[m, h], recv_sem.at[m, h],
        )
        dst[m, h, exp] = src[m, h, exp]

    def send_rows(src, dst, m, lines, send_sem, recv_sem):
        scatter(
            lambda p: src.at[m, p, lines], lambda p: dst.at[m, p, lines],
            send_sem.at[m], recv_sem.at[m],
        )
        dst[m, exp, lines] = src[m, exp, lines]

    def two_tiles(main):
        main = main.reshape(experts, 8, 4 * LANES)
        return [
            jnp.concatenate([main[:, :, c : c + LANES], main[:, :, c + LANES : c + 2 * LANES]], axis=1).astype(BF)
            for c in (0, 2 * LANES)
        ]

    def from_tiles(tiles):
        parts = []
        for t in tiles:
            t = t.astype(F32)
            parts.append(t[:, :8, :].reshape(experts * 8, LANES))
            parts.append(t[:, 8:, :].reshape(experts * 8, LANES))
        return jnp.concatenate(parts, axis=1).astype(BF)

    def to_slots(x, m, h, buf):
        tiles = two_tiles(dot(send_main[m], x))
        buf[m, h, :, 0:16, :] = tiles[0]
        buf[m, h, :, 16:32, :] = tiles[1]
        tail = dot(send_tail[m], stack_chunks(x))
        buf[m, h, :, 32:48, :] = tail.reshape(experts, 16, LANES).astype(BF)

    def to_rows(buf, m, h):
        cols = slice(512 * h, 512 * h + 512)
        rows[0 : experts * 8, cols] = from_tiles([buf[m, h, :, 0:16, :], buf[m, h, :, 16:32, :]])
        t = dot(perm[...], buf[m, h, :, 32:48, :].reshape(experts * 16, LANES))
        rows[experts * 8 : experts * 10, cols] = spread_chunks(t, experts * 2).astype(BF)

    def from_rows(product, m, buf, dst, send_sem, recv_sem):
        tails = []
        for h in range(2):
            res = product(slice(512 * h, 512 * h + 512))
            tiles = two_tiles(res[0 : experts * 8])
            buf[m, :, 32 * h : 32 * h + 16, :] = tiles[0]
            buf[m, :, 32 * h + 16 : 32 * h + 32, :] = tiles[1]
            tails.append(stack_chunks(res[experts * 8 : experts * 10].astype(BF)))
            if h == 0:
                send_rows(buf, dst, m, pl.ds(0, 32), send_sem, recv_sem)
        tail = dot(perm_t[...], jnp.concatenate(tails, axis=0))
        buf[m, :, 64:80, :] = tail.reshape(experts, 16, LANES).astype(BF)
        send_rows(buf, dst, m, pl.ds(32, 48), send_sem, recv_sem)

    def combine(buf, m, main_table, tail_table):
        tiles = [buf[m, :, 16 * q : 16 * q + 16, :] for q in range(4)]
        main = dot(main_table[m], from_tiles(tiles))
        tail = dot(tail_table[m], buf[m, :, 64:80, :].reshape(experts * 16, LANES))
        return main + spread_chunks(tail, toks)

    def grad_of(m):
        return jnp.concatenate([rz[m, 0], rz[m, 1]], axis=1)

    q = iota((256, 256), 0)
    r = iota((256, 256), 1)
    q_half = iota((128, 256), 0)
    picked = ((q_half & 31) >> 1) * 16 + (q_half & 1) * 4 + (q_half >> 5)
    perm[...] = (iota((128, 256), 1) == picked).astype(F32).astype(BF)
    picked_t = ((r & 31) >> 1) * 16 + (r & 1) * 8 + (r >> 5)
    perm_t[...] = (q == picked_t).astype(F32).astype(BF)
    eye[...] = (q == r).astype(F32).astype(BF)
    router_pad[...] = jnp.zeros_like(router_pad)
    router_pad[0:experts, :] = router_t[...]
    router_acc[...] = jnp.zeros_like(router_acc)
    gain_acc[...] = jnp.zeros_like(gain_acc)

    e_r = iota((experts, LANES), 0)

    def twice(line):
        return jnp.concatenate([line, line], axis=1)

    def code_lines(m):
        square = iota((experts, experts), 0) == iota((experts, experts), 1)
        limit = jnp.sum(jnp.where(square, caps[m].astype(F32), 0.0), axis=1, keepdims=True)
        found = []
        for k in range(2):
            chosen = twice(ids[m, k : k + 1, :])
            place = twice(places[m, k : k + 1, :])
            most = jnp.sum(jnp.where(e_r == chosen, limit, 0.0), axis=0, keepdims=True)
            found += [chosen, jnp.where(place.astype(F32) < most, chosen * 16 + place, -1)]
        return found

    def tokens_forward(m):
        x = acts[m].astype(F32)
        centred = x - jnp.mean(x, axis=-1, keepdims=True)
        inv = lax.rsqrt(jnp.mean(centred * centred, axis=-1, keepdims=True) + 1e-06)
        unit = centred * inv
        normed = (unit * gain[...]).astype(BF)
        unit_s[m] = unit
        inv_s[m] = jnp.broadcast_to(inv, (toks, LANES))
        normed_s[m] = normed
        _, code1, _, code2 = code_lines(m)
        slot_r = iota((128, LANES), 0)
        slot_code = (slot_r >> 3) * 16 + (slot_r & 7)
        hit = ((slot_code == code1) | (slot_code == code2)).astype(F32)
        send_main[m] = hit[:, :toks].astype(BF)
        wide1 = jnp.concatenate([code1] * 2, axis=1)
        wide2 = jnp.concatenate([code2] * 2, axis=1)
        tail_r = iota((256, 256), 0)
        tail_code = (tail_r >> 4) * 16 + 8 + ((tail_r >> 2) & 1)
        same = ((iota((256, 256), 1) >> 6) == (tail_r & 3)) & ((tail_r & 8) == 0)
        hit = (((tail_code == wide1) | (tail_code == wide2)) & same).astype(F32)
        send_tail[m] = hit.astype(BF)
        for h in range(2):
            to_slots(normed[:, 512 * h : 512 * h + 512], m, h, su)

    def tokens_tables(m):
        id1, code1, id2, code2 = code_lines(m)
        normed = normed_s[m]
        logits = dot(router_t[...], jnp.concatenate([normed, normed], axis=0), 1, 1)
        chosen1 = jnp.sum(jnp.where(e_r == id1, logits, 0.0), axis=0, keepdims=True)
        chosen2 = jnp.sum(jnp.where(e_r == id2, logits, 0.0), axis=0, keepdims=True)
        gate1 = 1.0 / (1.0 + jnp.exp(chosen2 - chosen1))
        gate2 = 1.0 - gate1
        line = iota((8, LANES), 0)
        lines = jnp.where(line == 0, code1.astype(F32), 0.0)
        lines = jnp.where(line == 1, code2.astype(F32), lines)
        lines = jnp.where(line == 2, id1.astype(F32), lines)
        lines = jnp.where(line == 3, id2.astype(F32), lines)
        lines = jnp.where(line == 4, gate1, lines)
        lines = jnp.where(line == 5, gate2, lines)
        lines = jnp.concatenate([lines, jnp.zeros((LANES - 8, LANES), F32)], axis=0)
        turned = jnp.transpose(lines)[:toks]
        c1 = turned[:, 0:1].astype(jnp.int32)
        c2 = turned[:, 1:2].astype(jnp.int32)
        i1 = turned[:, 2:3].astype(jnp.int32)
        i2 = turned[:, 3:4].astype(jnp.int32)
        g1 = turned[:, 4:5]
        g2 = turned[:, 5:6]
        e_l = iota((toks, LANES), 1)
        pdg_s[m] = g1 * g2 * ((e_l == i1).astype(F32) - (e_l == i2).astype(F32))
        slot_code = (e_l >> 3) * 16 + (e_l & 7)
        hit1 = (slot_code == c1).astype(F32)
        hit2 = (slot_code == c2).astype(F32)
        mix_main[m] = (g1 * hit1 + g2 * hit2).astype(BF)
        diff_main[m] = (hit1 - hit2).astype(BF)
        lane = iota((toks, 256), 1)
        tail_code = (lane >> 4) * 16 + 8 + ((lane >> 3) & 1)
        hit1 = (tail_code == c1).astype(F32)
        hit2 = (tail_code == c2).astype(F32)
        mixed = g1 * hit1 + g2 * hit2
        differ = hit1 - hit2
        for c in range(8):
            here = (lane & 7) == c
            mix_tail[m, toks * c : toks * c + toks, :] = jnp.where(here, mixed, 0.0).astype(BF)
            diff_tail[m, toks * c : toks * c + toks, :] = jnp.where(here, differ, 0.0).astype(BF)

    def experts_forward(m):
        for h in range(2):
            all_parts(ru, m, h, u_recv).wait()
            to_rows(ru, m, h)
        for n in range(4):
            cols = slice(1024 * n, 1024 * n + 1024)
            hidden = dot(rows[...], w_in[:, cols])
            square = hidden * hidden
            tanh = jnp.tanh(GELU_C * hidden * (1.0 + 0.044715 * square))
            rise = 0.5 * (1.0 + tanh)
            active[m, :, cols] = (hidden * rise).astype(BF)
            bend = 0.5 * hidden * (1.0 - tanh * tanh) * (GELU_C + (3.0 * 0.044715 * GELU_C) * square)
            slope[m, :, cols] = (rise + bend).astype(BF)

    def experts_value(m):
        from_rows(lambda cols: dot(active[m], w_out[:, cols]), m, sy, ry, y_send, y_recv)

    def tokens_value(m):
        all_rows(ry, m, y_recv).wait()
        ydiff_s[m] = combine(ry, m, diff_main, diff_tail)

    def tokens_send(m, h):
        to_slots(rz[m, h], m, h, sg)
        send_part(sg, rg, m, h, g_send, g_recv)

    def tokens_gate(m):
        dots = jnp.sum(ydiff_s[m] * grad_of(m).astype(F32), axis=1, keepdims=True)
        dlogits = (dots * pdg_s[m]).astype(BF)
        extra_s[m] = dot(dlogits, router_pad[...])
        router_acc[...] += dot(dlogits, normed_s[m], 0, 0)[:experts]

    def experts_backward(m, turned):
        def product(h):
            cols = slice(512 * h, 512 * h + 512)
            if turned:
                return dot(rows[:, cols], w_out_t[cols, :])
            return dot(rows[:, cols], w_out[:, cols], 1, 1)

        all_parts(rg, m, 0, g_recv).wait()
        to_rows(rg, m, 0)
        back_s[...] = product(0)
        all_parts(rg, m, 1, g_recv).wait()
        to_rows(rg, m, 1)
        pre[...] = ((back_s[...] + product(1)) * slope[m].astype(F32)).astype(BF)

    def experts_return(m, turned):
        def product(cols):
            if turned:
                return dot(pre[...], w_out[:, cols])
            return dot(pre[...], w_in[cols, :], 1, 1)

        from_rows(product, m, sr, rr, r_send, r_recv)

    def tokens_backward(m):
        all_rows(rr, m, r_recv).wait()
        unit = unit_s[m]
        norm_grad = combine(rr, m, mix_main, mix_tail) + extra_s[m]
        xhat = norm_grad * gain[...]
        mean1 = jnp.mean(xhat, axis=-1, keepdims=True)
        mean2 = jnp.mean(xhat * unit, axis=-1, keepdims=True)
        step = inv_s[m][:, 0:1] * (xhat - mean1 - unit * mean2)
        in_grad = (grad_of(m).astype(F32) + step).astype(BF)
        for h in range(2):
            sz[m, h] = in_grad[:, 512 * h : 512 * h + 512]

            @pl.when(sec > 0)
            def _():
                z_copy(m, h).start()

        o_grads[m] = in_grad
        terms = (norm_grad * unit).reshape(toks // 8, 8, width)
        gain_acc[...] += jnp.sum(terms, axis=0)

    def z_copy(m, h):
        return pltpu.make_async_remote_copy(
            src_ref=sz.at[m, h], dst_ref=rz.at[m, h],
            send_sem=z_send.at[m, h], recv_sem=z_recv.at[m, h],
            device_id=(jnp.maximum(sec - 1, 0), exp, core), device_id_type=MESH,
        )

    def tile(j):
        lines = slice(8 * (j // 8), 8 * (j // 8) + 8)
        return lines, slice(LANES * (j % 8), LANES * (j % 8) + LANES)

    def to_peers(src_of, dst, k):
        scatter(src_of, lambda p: dst.at[p], f_send.at[k], f_recv.at[k])

    def to_pair(src, dst, k):
        return pltpu.make_async_remote_copy(
            src_ref=src, dst_ref=dst, send_sem=f_send.at[k], recv_sem=f_recv.at[k],
            device_id=(sec, exp, 1 - core), device_id_type=MESH,
        )

    def all_but_one(buf, sem, k):
        return others(buf.at[pl.ds(0, experts - 1)], sem.at[k])

    def router_parts():
        for j in range(experts):
            lines, cols = tile(j)
            fin_s[j] = router_acc[lines, cols]
        to_peers(lambda p: fin_s.at[p], fin_r, 0)
        fin_r[exp] = fin_s[exp]

    def last_sums():
        gain_x[...] = jnp.sum(gain_acc[...], axis=0, keepdims=True)
        gain_pair = to_pair(gain_x, gain_y, 3)
        gain_pair.start()
        all_but_one(fin_r, f_recv, 0).wait()
        fin_x[...] = jnp.sum(fin_r[...], axis=0)
        pair = to_pair(fin_x, fin_y, 1)
        pair.start()
        gain_pair.wait()
        gain_t[...] = (gain_x[...] + gain_y[...]) * scale
        to_peers(lambda p: gain_t, gain_g, 4)
        gain_g[exp] = gain_t[...]
        pair.wait()
        fin_t[...] = (fin_x[...] + fin_y[...]) * scale
        to_peers(lambda p: fin_t, fin_g, 2)
        fin_g[exp] = fin_t[...]

    tokens_forward(0)

    @pl.when(sec == last)
    def _():
        for m in range(micros):
            for h in range(2):
                rz[m, h] = out_grad[m, :, 512 * h : 512 * h + 512]
        for h in range(2):
            to_slots(rz[0, h], 0, h, sg)

    @pl.when(sec > 0)
    def _():
        pl.semaphore_wait(barrier, experts + 1)

    @pl.when(sec == 0)
    def _():
        pl.semaphore_wait(barrier, experts)

    part_in.start()
    part_out.start()
    for h in range(2):
        send_part(su, ru, 0, h, u_send, u_recv)

    @pl.when(sec == last)
    def _():
        for h in range(2):
            send_part(sg, rg, 0, h, g_send, g_recv)

    tokens_tables(0)

    @pl.loop(1, micros)
    def _(m):
        tokens_forward(m)
        for h in range(2):
            send_part(su, ru, m, h, u_send, u_recv)

        @pl.when(sec == last)
        def _():
            for h in range(2):
                tokens_send(m, h)

        tokens_tables(m)

    own_in.wait()
    part_in.wait_recv()
    pl.loop(0, micros)(experts_forward)
    own_out.wait()
    part_out.wait_recv()

    @pl.when(sec == last)
    def _():
        @pl.loop(0, micros)
        def _(m):
            experts_value(m)

            @pl.when(m > 0)
            def _():
                tokens_value(m - 1)
                tokens_gate(m - 1)

            experts_backward(m, False)

            @pl.when(m > 0)
            def _():
                tokens_backward(m - 1)

            experts_return(m, False)

        tokens_value(micros - 1)
        tokens_gate(micros - 1)
        router_parts()

    @pl.when(sec < last)
    def _():
        pl.loop(0, micros)(experts_value)

        @pl.loop(0, width // 256)
        def _(n):
            lines = pl.ds(pl.multiple_of(n * 256, 256), 256)
            w_out_t[lines, :] = dot(eye[...], w_out[:, lines], 1, 1).astype(BF)

        @pl.loop(0, 2 * half // 256)
        def _(n):
            lines = pl.ds(pl.multiple_of(n * 256, 256), 256)
            w_out[lines, :] = dot(eye[...], w_in[:, lines], 1, 1).astype(BF)

        pl.loop(0, micros)(tokens_value)

        @pl.loop(0, micros)
        def _(m):
            for h in range(2):
                z_copy(m, h).wait_recv()
                tokens_send(m, h)
            tokens_gate(m)

            @pl.when(m > 0)
            def _():
                tokens_backward(m - 1)

            experts_backward(m, True)
            experts_return(m, True)

        router_parts()

    tokens_backward(micros - 1)
    last_sums()
    all_but_one(fin_g, f_recv, 2).wait()
    for j in range(experts):
        lines, cols = tile(j)
        o_router[lines, cols] = fin_g[j]
    all_but_one(gain_g, f_recv, 4).wait()
    o_gain[...] = jnp.sum(gain_g[...], axis=0)

    @pl.loop(0, micros)
    def _(m):
        all_rows(sy, m, y_send).wait()
        all_rows(sr, m, r_send).wait()
        for h in range(2):
            all_parts(su, m, h, u_send).wait()
            all_parts(sg, m, h, g_send).wait()

            @pl.when(sec > 0)
            def _():
                z_copy(m, h).wait_send()

    all_but_one(fin_r, f_send, 0).wait()
    all_but_one(fin_g, f_send, 2).wait()
    all_but_one(gain_g, f_send, 4).wait()
    part_in.wait_send()
    part_out.wait_send()


def copy_out(a, b, c, to_a, to_b, to_c):
    to_a[...] = a[...]
    to_b[...] = b[...]
    to_c[...] = c[...]


def per_device(acts, out_grad, ln_gain, router, w_in, w_out, expert_ids, slot_ids, capacity):
    _, micros, toks, width = acts.shape
    experts = router.shape[2]
    half = w_in.shape[3]
    cap_slots = 10
    slots = experts * cap_slots
    tokens_all = toks * lax.axis_size("expert") * lax.axis_size("dp")
    scale = 1.0 / math.sqrt(micros * tokens_all)
    ids = jnp.transpose(expert_ids[0], (0, 2, 1))
    places = jnp.transpose(slot_ids[0], (0, 2, 1))
    caps = jnp.transpose(capacity, (1, 0, 2))
    vmem = pl.BlockSpec(memory_space=pltpu.VMEM)
    hbm = pl.BlockSpec(memory_space=pl.ANY)
    dma = pltpu.SemaphoreType.DMA
    grads, gain_out, router_out = pl.pallas_call(
        functools.partial(kernel, scale=scale),
        out_shape=(
            jax.ShapeDtypeStruct((micros, toks, width), BF),
            jax.ShapeDtypeStruct((1, width), F32),
            jax.ShapeDtypeStruct((experts, width), F32),
        ),
        in_specs=[vmem] * 7 + [hbm] * 2,
        out_specs=(vmem, vmem, vmem),
        scratch_shapes=[
            pltpu.VMEM((width, 2 * half), BF),
            pltpu.VMEM((2 * half, width), BF),
            pltpu.VMEM((width, 2 * half), BF),
            pltpu.VMEM((micros, slots, 2 * half), BF),
            pltpu.VMEM((micros, slots, 2 * half), BF),
            pltpu.VMEM((slots, 2 * half), BF),
            pltpu.VMEM((slots, width), BF),
            pltpu.VMEM((slots, 2 * half), F32),
        ]
        + [pltpu.VMEM((micros, 2, experts, 48, LANES), BF)] * 4
        + [pltpu.VMEM((micros, experts, 80, LANES), BF)] * 4
        + [pltpu.VMEM((micros, 2, toks, width // 2), BF)] * 2
        + [
            pltpu.VMEM((micros, toks, width), F32),
            pltpu.VMEM((micros, toks, LANES), F32),
            pltpu.VMEM((micros, toks, width), BF),
            pltpu.VMEM((micros, toks, width), F32),
            pltpu.VMEM((micros, toks, width), F32),
            pltpu.VMEM((micros, toks, LANES), F32),
            pltpu.VMEM((micros, 128, toks), BF),
            pltpu.VMEM((micros, 256, 256), BF),
            pltpu.VMEM((micros, toks, 128), BF),
            pltpu.VMEM((micros, 512, 256), BF),
            pltpu.VMEM((micros, toks, 128), BF),
            pltpu.VMEM((micros, 512, 256), BF),
            pltpu.VMEM((LANES, width), BF),
            pltpu.VMEM((128, 256), BF),
            pltpu.VMEM((256, 256), BF),
            pltpu.VMEM((256, 256), BF),
            pltpu.VMEM((experts, width), F32),
            pltpu.VMEM((8, width), F32),
            pltpu.VMEM((experts, 8, LANES), F32),
            pltpu.VMEM((experts, 8, LANES), F32),
            pltpu.VMEM((8, LANES), F32),
            pltpu.VMEM((8, LANES), F32),
            pltpu.VMEM((8, LANES), F32),
            pltpu.VMEM((experts, 8, LANES), F32),
            pltpu.VMEM((1, width), F32),
            pltpu.VMEM((1, width), F32),
            pltpu.VMEM((1, width), F32),
            pltpu.VMEM((experts, 1, width), F32),
            dma((2,)),
            dma((2,)),
            dma((2,)),
        ]
        + [dma((micros, 2))] * 6
        + [dma((micros,))] * 4
        + [dma((5,))] * 2,
        compiler_params=pltpu.CompilerParams(
            collective_id=0, has_side_effects=True, vmem_limit_bytes=60 * 2**20
        ),
    )(
        acts[0],
        out_grad,
        ln_gain,
        jnp.transpose(router[0]),
        ids,
        places,
        caps,
        w_in[0, 0],
        w_out[0, 0],
    )
    grads, gain_out, router_out = pl.pallas_call(
        copy_out,
        out_shape=(
            jax.ShapeDtypeStruct((micros, toks, width), BF),
            jax.ShapeDtypeStruct((1, width), F32),
            jax.ShapeDtypeStruct((experts, width), F32),
        ),
        in_specs=[vmem] * 3,
        out_specs=(vmem, vmem, vmem),
    )(grads, gain_out, router_out)
    return (grads[None], gain_out, jnp.transpose(router_out)[None])


def solution(mesh):
    return jax.shard_map(
        per_device,
        mesh=mesh,
        in_specs=(
            P("section", None, ("expert", "dp"), None),
            P(None, ("expert", "dp"), None),
            P("section", None),
            P("section", None, None),
            P("section", "expert", None, "dp"),
            P("section", "expert", "dp", None),
            P("section", None, ("expert", "dp"), None),
            P("section", None, ("expert", "dp"), None),
            P("section", None, None),
        ),
        out_specs=(
            P("section", None, ("expert", "dp"), None),
            P("section", None),
            P("section", None, None),
        ),
        check_vma=False,
    )
```

```python
import functools
import math

import jax
import jax.numpy as jnp
from jax import lax
from jax.experimental import pallas as pl
from jax.experimental.pallas import tpu as pltpu
from jax.sharding import PartitionSpec as P

GELU_C = math.sqrt(2.0 / math.pi)
MESH = pl.DeviceIdType.MESH
BF = jnp.bfloat16
F32 = jnp.float32
SIDE = 4
LANES = 128


def plane_offsets():
    offs = [(k // SIDE, k % SIDE) for k in range(1, SIDE * SIDE)]
    far = lambda o: min(o[0], SIDE - o[0]) + min(o[1], SIDE - o[1])
    return sorted(offs, key=lambda o: -far(o))


def dot(a, b, ca=1, cb=0):
    return lax.dot_general(a, b, (((ca,), (cb,)), ((), ())), preferred_element_type=F32)


def iota(shape, dim):
    return lax.broadcasted_iota(jnp.int32, shape, dim)


def stack_chunks(x):
    return jnp.concatenate([x[:, c : c + LANES] for c in range(0, x.shape[1], LANES)], axis=0)


def spread_chunks(x, rows):
    return jnp.concatenate([x[r : r + rows] for r in range(0, x.shape[0], rows)], axis=1)


def kernel(
    acts, out_grad, gain, router_t, ids, places, caps, w_in_own, w_out_own,
    o_grads, o_gain, o_router,
    w_in, w_out, w_out_t, slope, active, pre, rows, back_s,
    su, ru, sg, rg, sy, ry, sr, rr, rz, sz,
    unit_s, inv_s, normed_s, ydiff_s, extra_s, pdg_s,
    send_main, send_tail, mix_main, mix_tail, diff_main, diff_tail,
    router_pad, perm, perm_t, eye, router_acc, gain_acc,
    fin_s, fin_r, fin_x, fin_y, fin_t, fin_g, gain_x, gain_y, gain_t, gain_g,
    w_local, w_send, w_recv,
    u_send, u_recv, g_send, g_recv, z_send, z_recv, y_send, y_recv, r_send, r_recv,
    f_send, f_recv,
    *, scale,
):
    sec = lax.axis_index("section")
    exp = lax.axis_index("expert")
    core = lax.axis_index("dp")
    sections = lax.axis_size("section")
    last = sections - 1
    col = exp // SIDE
    row = lax.rem(exp, SIDE)
    peers = [
        lax.rem(col + dy, SIDE) * SIDE + lax.rem(row + dx, SIDE) for dy, dx in plane_offsets()
    ]
    experts = SIDE * SIDE
    micros = acts.shape[0]
    toks = acts.shape[1]
    width = acts.shape[2]
    half = w_in_own.shape[1]

    own_in = pltpu.make_async_copy(w_in_own, w_in.at[:, pl.ds(0, half)], w_local.at[0])
    own_out = pltpu.make_async_copy(w_out_own, w_out.at[pl.ds(0, half), :], w_local.at[1])
    own_in.start()
    own_out.start()

    barrier = pltpu.get_barrier_semaphore()
    for p in peers:
        pl.semaphore_signal(barrier, inc=1, device_id=(sec, p, core), device_id_type=MESH)
    pl.semaphore_signal(barrier, inc=1, device_id=(sec, exp, 1 - core), device_id_type=MESH)

    @pl.when(sec < last)
    def _():
        pl.semaphore_signal(barrier, inc=1, device_id=(sec + 1, exp, core), device_id_type=MESH)

    part_in = pltpu.make_async_remote_copy(
        src_ref=w_in_own, dst_ref=w_in.at[:, pl.ds(half, half)],
        send_sem=w_send.at[0], recv_sem=w_recv.at[0],
        device_id=(sec, exp, 1 - core), device_id_type=MESH,
    )
    part_out = pltpu.make_async_remote_copy(
        src_ref=w_out_own, dst_ref=w_out.at[pl.ds(half, half), :],
        send_sem=w_send.at[1], recv_sem=w_recv.at[1],
        device_id=(sec, exp, 1 - core), device_id_type=MESH,
    )

    def scatter(src_of, dst_of, send_sem, recv_sem):
        for p in peers:
            pltpu.make_async_remote_copy(
                src_ref=src_of(p), dst_ref=dst_of(exp), send_sem=send_sem, recv_sem=recv_sem,
                device_id=(sec, p, core), device_id_type=MESH,
            ).start()

    def others(part, sem):
        return pltpu.make_async_copy(part, part, sem)

    def all_parts(buf, m, h, sem):
        return others(buf.at[m, h, pl.ds(0, experts - 1)], sem.at[m, h])

    def all_rows(buf, m, sem):
        return others(buf.at[m, pl.ds(0, experts - 1)], sem.at[m])

    def send_part(src, dst, m, h, send_sem, recv_sem):
        scatter(
            lambda p: src.at[m, h, p], lambda p: dst.at[m, h, p],
            send_sem.at[m, h], recv_sem.at[m, h],
        )
        dst[m, h, exp] = src[m, h, exp]

    def send_rows(src, dst, m, lines, send_sem, recv_sem):
        scatter(
            lambda p: src.at[m, p, lines], lambda p: dst.at[m, p, lines],
            send_sem.at[m], recv_sem.at[m],
        )
        dst[m, exp, lines] = src[m, exp, lines]

    def two_tiles(main):
        main = main.reshape(experts, 8, 4 * LANES)
        return [
            jnp.concatenate([main[:, :, c : c + LANES], main[:, :, c + LANES : c + 2 * LANES]], axis=1).astype(BF)
            for c in (0, 2 * LANES)
        ]

    def from_tiles(tiles):
        parts = []
        for t in tiles:
            t = t.astype(F32)
            parts.append(t[:, :8, :].reshape(experts * 8, LANES))
            parts.append(t[:, 8:, :].reshape(experts * 8, LANES))
        return jnp.concatenate(parts, axis=1).astype(BF)

    def to_slots(x, m, h, buf):
        tiles = two_tiles(dot(send_main[m], x))
        buf[m, h, :, 0:16, :] = tiles[0]
        buf[m, h, :, 16:32, :] = tiles[1]
        tail = dot(send_tail[m], stack_chunks(x))
        buf[m, h, :, 32:48, :] = tail.reshape(experts, 16, LANES).astype(BF)

    def to_rows(buf, m, h):
        cols = slice(512 * h, 512 * h + 512)
        rows[0 : experts * 8, cols] = from_tiles([buf[m, h, :, 0:16, :], buf[m, h, :, 16:32, :]])
        t = dot(perm[...], buf[m, h, :, 32:48, :].reshape(experts * 16, LANES))
        rows[experts * 8 : experts * 10, cols] = spread_chunks(t, experts * 2).astype(BF)

    def from_rows(product, m, buf, dst, send_sem, recv_sem):
        tails = []
        for h in range(2):
            res = product(slice(512 * h, 512 * h + 512))
            tiles = two_tiles(res[0 : experts * 8])
            buf[m, :, 32 * h : 32 * h + 16, :] = tiles[0]
            buf[m, :, 32 * h + 16 : 32 * h + 32, :] = tiles[1]
            tails.append(stack_chunks(res[experts * 8 : experts * 10].astype(BF)))
            if h == 0:
                send_rows(buf, dst, m, pl.ds(0, 32), send_sem, recv_sem)
        tail = dot(perm_t[...], jnp.concatenate(tails, axis=0))
        buf[m, :, 64:80, :] = tail.reshape(experts, 16, LANES).astype(BF)
        send_rows(buf, dst, m, pl.ds(32, 48), send_sem, recv_sem)

    def combine(buf, m, main_table, tail_table):
        tiles = [buf[m, :, 16 * q : 16 * q + 16, :] for q in range(4)]
        main = dot(main_table[m], from_tiles(tiles))
        tail = dot(tail_table[m], buf[m, :, 64:80, :].reshape(experts * 16, LANES))
        return main + spread_chunks(tail, toks)

    def grad_of(m):
        return jnp.concatenate([rz[m, 0], rz[m, 1]], axis=1)

    q = iota((256, 256), 0)
    r = iota((256, 256), 1)
    q_half = iota((128, 256), 0)
    picked = ((q_half & 31) >> 1) * 16 + (q_half & 1) * 4 + (q_half >> 5)
    perm[...] = (iota((128, 256), 1) == picked).astype(F32).astype(BF)
    picked_t = ((r & 31) >> 1) * 16 + (r & 1) * 8 + (r >> 5)
    perm_t[...] = (q == picked_t).astype(F32).astype(BF)
    eye[...] = (q == r).astype(F32).astype(BF)
    router_pad[...] = jnp.zeros_like(router_pad)
    router_pad[0:experts, :] = router_t[...]
    router_acc[...] = jnp.zeros_like(router_acc)
    gain_acc[...] = jnp.zeros_like(gain_acc)

    e_r = iota((experts, LANES), 0)

    def twice(line):
        return jnp.concatenate([line, line], axis=1)

    def code_lines(m):
        square = iota((experts, experts), 0) == iota((experts, experts), 1)
        limit = jnp.sum(jnp.where(square, caps[m].astype(F32), 0.0), axis=1, keepdims=True)
        found = []
        for k in range(2):
            chosen = twice(ids[m, k : k + 1, :])
            place = twice(places[m, k : k + 1, :])
            most = jnp.sum(jnp.where(e_r == chosen, limit, 0.0), axis=0, keepdims=True)
            found += [chosen, jnp.where(place.astype(F32) < most, chosen * 16 + place, -1)]
        return found

    def tokens_forward(m):
        x = acts[m].astype(F32)
        centred = x - jnp.mean(x, axis=-1, keepdims=True)
        inv = lax.rsqrt(jnp.mean(centred * centred, axis=-1, keepdims=True) + 1e-06)
        unit = centred * inv
        normed = (unit * gain[...]).astype(BF)
        unit_s[m] = unit
        inv_s[m] = jnp.broadcast_to(inv, (toks, LANES))
        normed_s[m] = normed
        _, code1, _, code2 = code_lines(m)
        slot_r = iota((128, LANES), 0)
        slot_code = (slot_r >> 3) * 16 + (slot_r & 7)
        hit = ((slot_code == code1) | (slot_code == code2)).astype(F32)
        send_main[m] = hit[:, :toks].astype(BF)
        wide1 = jnp.concatenate([code1] * 2, axis=1)
        wide2 = jnp.concatenate([code2] * 2, axis=1)
        tail_r = iota((256, 256), 0)
        tail_code = (tail_r >> 4) * 16 + 8 + ((tail_r >> 2) & 1)
        same = ((iota((256, 256), 1) >> 6) == (tail_r & 3)) & ((tail_r & 8) == 0)
        hit = (((tail_code == wide1) | (tail_code == wide2)) & same).astype(F32)
        send_tail[m] = hit.astype(BF)
        for h in range(2):
            to_slots(normed[:, 512 * h : 512 * h + 512], m, h, su)

    def tokens_tables(m):
        id1, code1, id2, code2 = code_lines(m)
        normed = normed_s[m]
        logits = dot(router_t[...], jnp.concatenate([normed, normed], axis=0), 1, 1)
        chosen1 = jnp.sum(jnp.where(e_r == id1, logits, 0.0), axis=0, keepdims=True)
        chosen2 = jnp.sum(jnp.where(e_r == id2, logits, 0.0), axis=0, keepdims=True)
        gate1 = 1.0 / (1.0 + jnp.exp(chosen2 - chosen1))
        gate2 = 1.0 - gate1
        line = iota((8, LANES), 0)
        lines = jnp.where(line == 0, code1.astype(F32), 0.0)
        lines = jnp.where(line == 1, code2.astype(F32), lines)
        lines = jnp.where(line == 2, id1.astype(F32), lines)
        lines = jnp.where(line == 3, id2.astype(F32), lines)
        lines = jnp.where(line == 4, gate1, lines)
        lines = jnp.where(line == 5, gate2, lines)
        lines = jnp.concatenate([lines, jnp.zeros((LANES - 8, LANES), F32)], axis=0)
        turned = jnp.transpose(lines)[:toks]
        c1 = turned[:, 0:1].astype(jnp.int32)
        c2 = turned[:, 1:2].astype(jnp.int32)
        i1 = turned[:, 2:3].astype(jnp.int32)
        i2 = turned[:, 3:4].astype(jnp.int32)
        g1 = turned[:, 4:5]
        g2 = turned[:, 5:6]
        e_l = iota((toks, LANES), 1)
        pdg_s[m] = g1 * g2 * ((e_l == i1).astype(F32) - (e_l == i2).astype(F32))
        slot_code = (e_l >> 3) * 16 + (e_l & 7)
        hit1 = (slot_code == c1).astype(F32)
        hit2 = (slot_code == c2).astype(F32)
        mix_main[m] = (g1 * hit1 + g2 * hit2).astype(BF)
        diff_main[m] = (hit1 - hit2).astype(BF)
        lane = iota((toks, 256), 1)
        tail_code = (lane >> 4) * 16 + 8 + ((lane >> 3) & 1)
        hit1 = (tail_code == c1).astype(F32)
        hit2 = (tail_code == c2).astype(F32)
        mixed = g1 * hit1 + g2 * hit2
        differ = hit1 - hit2
        for c in range(8):
            here = (lane & 7) == c
            mix_tail[m, toks * c : toks * c + toks, :] = jnp.where(here, mixed, 0.0).astype(BF)
            diff_tail[m, toks * c : toks * c + toks, :] = jnp.where(here, differ, 0.0).astype(BF)

    def experts_forward(m):
        for h in range(2):
            all_parts(ru, m, h, u_recv).wait()
            to_rows(ru, m, h)
        for n in range(4):
            cols = slice(1024 * n, 1024 * n + 1024)
            hidden = dot(rows[...], w_in[:, cols])
            square = hidden * hidden
            tanh = jnp.tanh(GELU_C * hidden * (1.0 + 0.044715 * square))
            rise = 0.5 * (1.0 + tanh)
            active[m, :, cols] = (hidden * rise).astype(BF)
            bend = 0.5 * hidden * (1.0 - tanh * tanh) * (GELU_C + (3.0 * 0.044715 * GELU_C) * square)
            slope[m, :, cols] = (rise + bend).astype(BF)

    def experts_value(m):
        from_rows(lambda cols: dot(active[m], w_out[:, cols]), m, sy, ry, y_send, y_recv)

    def tokens_value(m):
        all_rows(ry, m, y_recv).wait()
        ydiff_s[m] = combine(ry, m, diff_main, diff_tail)

    def tokens_send(m, h):
        to_slots(rz[m, h], m, h, sg)
        send_part(sg, rg, m, h, g_send, g_recv)

    def tokens_gate(m):
        dots = jnp.sum(ydiff_s[m] * grad_of(m).astype(F32), axis=1, keepdims=True)
        dlogits = (dots * pdg_s[m]).astype(BF)
        extra_s[m] = dot(dlogits, router_pad[...])
        router_acc[...] += dot(dlogits, normed_s[m], 0, 0)[:experts]

    def experts_backward(m, turned):
        def product(h):
            cols = slice(512 * h, 512 * h + 512)
            if turned:
                return dot(rows[:, cols], w_out_t[cols, :])
            return dot(rows[:, cols], w_out[:, cols], 1, 1)

        all_parts(rg, m, 0, g_recv).wait()
        to_rows(rg, m, 0)
        back_s[...] = product(0)
        all_parts(rg, m, 1, g_recv).wait()
        to_rows(rg, m, 1)
        pre[...] = ((back_s[...] + product(1)) * slope[m].astype(F32)).astype(BF)

    def experts_return(m, turned):
        def product(cols):
            if turned:
                return dot(pre[...], w_out[:, cols])
            return dot(pre[...], w_in[cols, :], 1, 1)

        from_rows(product, m, sr, rr, r_send, r_recv)

    def tokens_backward(m):
        all_rows(rr, m, r_recv).wait()
        unit = unit_s[m]
        norm_grad = combine(rr, m, mix_main, mix_tail) + extra_s[m]
        xhat = norm_grad * gain[...]
        mean1 = jnp.mean(xhat, axis=-1, keepdims=True)
        mean2 = jnp.mean(xhat * unit, axis=-1, keepdims=True)
        step = inv_s[m][:, 0:1] * (xhat - mean1 - unit * mean2)
        in_grad = (grad_of(m).astype(F32) + step).astype(BF)
        for h in range(2):
            sz[m, h] = in_grad[:, 512 * h : 512 * h + 512]

            @pl.when(sec > 0)
            def _():
                z_copy(m, h).start()

        o_grads[m] = in_grad
        terms = (norm_grad * unit).reshape(toks // 8, 8, width)
        gain_acc[...] += jnp.sum(terms, axis=0)

    def z_copy(m, h):
        return pltpu.make_async_remote_copy(
            src_ref=sz.at[m, h], dst_ref=rz.at[m, h],
            send_sem=z_send.at[m, h], recv_sem=z_recv.at[m, h],
            device_id=(jnp.maximum(sec - 1, 0), exp, core), device_id_type=MESH,
        )

    def tile(j):
        lines = slice(8 * (j // 8), 8 * (j // 8) + 8)
        return lines, slice(LANES * (j % 8), LANES * (j % 8) + LANES)

    def to_peers(src_of, dst, k):
        scatter(src_of, lambda p: dst.at[p], f_send.at[k], f_recv.at[k])

    def to_pair(src, dst, k):
        return pltpu.make_async_remote_copy(
            src_ref=src, dst_ref=dst, send_sem=f_send.at[k], recv_sem=f_recv.at[k],
            device_id=(sec, exp, 1 - core), device_id_type=MESH,
        )

    def all_but_one(buf, sem, k):
        return others(buf.at[pl.ds(0, experts - 1)], sem.at[k])

    def router_parts():
        for j in range(experts):
            lines, cols = tile(j)
            fin_s[j] = router_acc[lines, cols]
        to_peers(lambda p: fin_s.at[p], fin_r, 0)
        fin_r[exp] = fin_s[exp]

    def router_sums():
        all_but_one(fin_r, f_recv, 0).wait()
        fin_x[...] = jnp.sum(fin_r[...], axis=0)
        pair = to_pair(fin_x, fin_y, 1)
        pair.start()
        pair.wait()
        fin_t[...] = (fin_x[...] + fin_y[...]) * scale
        to_peers(lambda p: fin_t, fin_g, 2)
        fin_g[exp] = fin_t[...]

    def gain_sums():
        gain_x[...] = jnp.sum(gain_acc[...], axis=0, keepdims=True)
        pair = to_pair(gain_x, gain_y, 3)
        pair.start()
        pair.wait()
        gain_t[...] = (gain_x[...] + gain_y[...]) * scale
        to_peers(lambda p: gain_t, gain_g, 4)
        gain_g[exp] = gain_t[...]

    tokens_forward(0)

    @pl.when(sec == last)
    def _():
        for m in range(micros):
            for h in range(2):
                rz[m, h] = out_grad[m, :, 512 * h : 512 * h + 512]
        for h in range(2):
            to_slots(rz[0, h], 0, h, sg)

    @pl.when(sec > 0)
    def _():
        pl.semaphore_wait(barrier, experts + 1)

    @pl.when(sec == 0)
    def _():
        pl.semaphore_wait(barrier, experts)

    part_in.start()
    part_out.start()
    for h in range(2):
        send_part(su, ru, 0, h, u_send, u_recv)

    @pl.when(sec == last)
    def _():
        for h in range(2):
            send_part(sg, rg, 0, h, g_send, g_recv)

    tokens_tables(0)

    @pl.loop(1, micros)
    def _(m):
        tokens_forward(m)
        for h in range(2):
            send_part(su, ru, m, h, u_send, u_recv)

        @pl.when(sec == last)
        def _():
            for h in range(2):
                tokens_send(m, h)

        tokens_tables(m)

    own_in.wait()
    part_in.wait_recv()
    pl.loop(0, micros)(experts_forward)
    own_out.wait()
    part_out.wait_recv()

    @pl.when(sec == last)
    def _():
        @pl.loop(0, micros)
        def _(m):
            experts_value(m)

            @pl.when(m > 0)
            def _():
                tokens_value(m - 1)
                tokens_gate(m - 1)

            experts_backward(m, False)

            @pl.when(m > 0)
            def _():
                tokens_backward(m - 1)

            experts_return(m, False)

        tokens_value(micros - 1)
        tokens_gate(micros - 1)

    @pl.when(sec < last)
    def _():
        pl.loop(0, micros)(experts_value)

        @pl.loop(0, width // 256)
        def _(n):
            lines = pl.ds(pl.multiple_of(n * 256, 256), 256)
            w_out_t[lines, :] = dot(eye[...], w_out[:, lines], 1, 1).astype(BF)

        @pl.loop(0, 2 * half // 256)
        def _(n):
            lines = pl.ds(pl.multiple_of(n * 256, 256), 256)
            w_out[lines, :] = dot(eye[...], w_in[:, lines], 1, 1).astype(BF)

        pl.loop(0, micros)(tokens_value)

        @pl.loop(0, micros)
        def _(m):
            for h in range(2):
                z_copy(m, h).wait_recv()
                tokens_send(m, h)
            tokens_gate(m)

            @pl.when(m > 0)
            def _():
                tokens_backward(m - 1)

            @pl.when((m == micros - 1) & (sec == 0))
            def _():
                router_parts()

            experts_backward(m, True)
            experts_return(m, True)

    @pl.when(sec == 0)
    def _():
        router_sums()

    tokens_backward(micros - 1)

    @pl.when(sec > 0)
    def _():
        router_parts()
        router_sums()

    gain_sums()
    all_but_one(fin_g, f_recv, 2).wait()
    for j in range(experts):
        lines, cols = tile(j)
        o_router[lines, cols] = fin_g[j]
    all_but_one(gain_g, f_recv, 4).wait()
    o_gain[...] = jnp.sum(gain_g[...], axis=0)

    @pl.loop(0, micros)
    def _(m):
        all_rows(sy, m, y_send).wait()
        all_rows(sr, m, r_send).wait()
        for h in range(2):
            all_parts(su, m, h, u_send).wait()
            all_parts(sg, m, h, g_send).wait()

            @pl.when(sec > 0)
            def _():
                z_copy(m, h).wait_send()

    all_but_one(fin_r, f_send, 0).wait()
    all_but_one(fin_g, f_send, 2).wait()
    all_but_one(gain_g, f_send, 4).wait()
    part_in.wait_send()
    part_out.wait_send()


def copy_out(a, b, c, to_a, to_b, to_c):
    to_a[...] = a[...]
    to_b[...] = b[...]
    to_c[...] = c[...]


def per_device(acts, out_grad, ln_gain, router, w_in, w_out, expert_ids, slot_ids, capacity):
    _, micros, toks, width = acts.shape
    experts = router.shape[2]
    half = w_in.shape[3]
    cap_slots = 10
    slots = experts * cap_slots
    tokens_all = toks * lax.axis_size("expert") * lax.axis_size("dp")
    scale = 1.0 / math.sqrt(micros * tokens_all)
    ids = jnp.transpose(expert_ids[0], (0, 2, 1))
    places = jnp.transpose(slot_ids[0], (0, 2, 1))
    caps = jnp.transpose(capacity, (1, 0, 2))
    vmem = pl.BlockSpec(memory_space=pltpu.VMEM)
    hbm = pl.BlockSpec(memory_space=pl.ANY)
    dma = pltpu.SemaphoreType.DMA
    grads, gain_out, router_out = pl.pallas_call(
        functools.partial(kernel, scale=scale),
        out_shape=(
            jax.ShapeDtypeStruct((micros, toks, width), BF),
            jax.ShapeDtypeStruct((1, width), F32),
            jax.ShapeDtypeStruct((experts, width), F32),
        ),
        in_specs=[vmem] * 7 + [hbm] * 2,
        out_specs=(vmem, vmem, vmem),
        scratch_shapes=[
            pltpu.VMEM((width, 2 * half), BF),
            pltpu.VMEM((2 * half, width), BF),
            pltpu.VMEM((width, 2 * half), BF),
            pltpu.VMEM((micros, slots, 2 * half), BF),
            pltpu.VMEM((micros, slots, 2 * half), BF),
            pltpu.VMEM((slots, 2 * half), BF),
            pltpu.VMEM((slots, width), BF),
            pltpu.VMEM((slots, 2 * half), F32),
        ]
        + [pltpu.VMEM((micros, 2, experts, 48, LANES), BF)] * 4
        + [pltpu.VMEM((micros, experts, 80, LANES), BF)] * 4
        + [pltpu.VMEM((micros, 2, toks, width // 2), BF)] * 2
        + [
            pltpu.VMEM((micros, toks, width), F32),
            pltpu.VMEM((micros, toks, LANES), F32),
            pltpu.VMEM((micros, toks, width), BF),
            pltpu.VMEM((micros, toks, width), F32),
            pltpu.VMEM((micros, toks, width), F32),
            pltpu.VMEM((micros, toks, LANES), F32),
            pltpu.VMEM((micros, 128, toks), BF),
            pltpu.VMEM((micros, 256, 256), BF),
            pltpu.VMEM((micros, toks, 128), BF),
            pltpu.VMEM((micros, 512, 256), BF),
            pltpu.VMEM((micros, toks, 128), BF),
            pltpu.VMEM((micros, 512, 256), BF),
            pltpu.VMEM((LANES, width), BF),
            pltpu.VMEM((128, 256), BF),
            pltpu.VMEM((256, 256), BF),
            pltpu.VMEM((256, 256), BF),
            pltpu.VMEM((experts, width), F32),
            pltpu.VMEM((8, width), F32),
            pltpu.VMEM((experts, 8, LANES), F32),
            pltpu.VMEM((experts, 8, LANES), F32),
            pltpu.VMEM((8, LANES), F32),
            pltpu.VMEM((8, LANES), F32),
            pltpu.VMEM((8, LANES), F32),
            pltpu.VMEM((experts, 8, LANES), F32),
            pltpu.VMEM((1, width), F32),
            pltpu.VMEM((1, width), F32),
            pltpu.VMEM((1, width), F32),
            pltpu.VMEM((experts, 1, width), F32),
            dma((2,)),
            dma((2,)),
            dma((2,)),
        ]
        + [dma((micros, 2))] * 6
        + [dma((micros,))] * 4
        + [dma((5,))] * 2,
        compiler_params=pltpu.CompilerParams(
            collective_id=0, has_side_effects=True, vmem_limit_bytes=60 * 2**20
        ),
    )(
        acts[0],
        out_grad,
        ln_gain,
        jnp.transpose(router[0]),
        ids,
        places,
        caps,
        w_in[0, 0],
        w_out[0, 0],
    )
    grads, gain_out, router_out = pl.pallas_call(
        copy_out,
        out_shape=(
            jax.ShapeDtypeStruct((micros, toks, width), BF),
            jax.ShapeDtypeStruct((1, width), F32),
            jax.ShapeDtypeStruct((experts, width), F32),
        ),
        in_specs=[vmem] * 3,
        out_specs=(vmem, vmem, vmem),
    )(grads, gain_out, router_out)
    return (grads[None], gain_out, jnp.transpose(router_out)[None])


def solution(mesh):
    return jax.shard_map(
        per_device,
        mesh=mesh,
        in_specs=(
            P("section", None, ("expert", "dp"), None),
            P(None, ("expert", "dp"), None),
            P("section", None),
            P("section", None, None),
            P("section", "expert", None, "dp"),
            P("section", "expert", "dp", None),
            P("section", None, ("expert", "dp"), None),
            P("section", None, ("expert", "dp"), None),
            P("section", None, None),
        ),
        out_specs=(
            P("section", None, ("expert", "dp"), None),
            P("section", None),
            P("section", None, None),
        ),
        check_vma=False,
    )
```
